256 devices in a mesh: dp: 16 (over y, x), expert: 16 (over z, core).
Axes of the slice: x: 4, y: 4, z: 8, core: 2. Of those that a mesh axis runs over, the one named last changes fastest.
Arguments:
- queries: bfloat16 [65536, 4096], P(('dp', 'expert')), may hold values from -6 to 6
- key_rows: bfloat16 [65536, 4096], P(('dp', 'expert')), may hold values from -6 to 6
- value_rows: bfloat16 [65536, 4096], P(('dp', 'expert')), may hold values from -6 to 6
- slopes: float32 [32], replicated, may hold values from 0.002 to 0.1
- norm_gain: float32 [4096], replicated, may hold values from 0.5 to 1.5
- parents: int32 [256], P('dp'), may hold values from 0 to 31
- lengths: int32 [256], P('dp'), may hold values from 1 to 256, 32768 in all
- parent_states: float32 [32, 32, 128, 128], P('dp', 'expert'), may hold values from -96 to 96
Outputs:
- mixed: bfloat16 [65536, 4096], P(('dp', 'expert'))
- child_states: float32 [256, 32, 128, 128], P('dp', 'expert')
The draws below stay inside these ranges and needn't reach their ends.
Inputs may be any that keep to these rules, and one draw needn't show every extreme that they name: `parents`: index of the parent whose state the child continues. `lengths`: slots past a child's length are padding.
All inputs are finite; a program needn't handle non-finite values. No bound on the sum of `lengths` on one device may be relied on, other than what follows from the above.
Results may differ from the reference program's by a relative error of at most 0.0065.
Values may be sent and summed in bfloat16 or wider, within the bound.
A program may use at most 128 MiB of HBM per device.

```python
import math
import jax
import jax.numpy as jnp
import numpy as np
from jax import lax

HEADS = 32
HDIM = 128
SEG = 256
CH = 256
PARENTS = 32
ROWS = 65536


def place_ends(result, key, least, top_value):
    longest = result.shape.index(max(result.shape))
    spots = []
    for shift in (0, 1):
        where = [jax.random.randint(jax.random.fold_in(key, axis), (), 0, length) for axis, length in enumerate(result.shape)]
        where[longest] = (where[longest] + shift) % result.shape[longest]
        spots.append(tuple(where))
    return result.at[spots[0]].set(least).at[spots[1]].set(top_value)


def block_scale(key, shape, shards, least, high):
    def one(axis_at, shards_of):
        steps = jax.random.uniform(jax.random.fold_in(jax.random.fold_in(key, 6), axis_at), (shards_of,), jnp.float32, least / len(shards), high / len(shards))
        return jnp.repeat(jnp.exp(steps), shape[axis_at] // shards_of).reshape((-1,) + (1,) * (len(shape) - axis_at - 1))

    level = one(*shards[0])
    for cut in shards[1:]:
        level = level * one(*cut)
    return level


def rank_bounds(amount, slope):
    portions = [(1 << 20) // math.isqrt(standing ** slope) + 1 for standing in range(1, amount + 1)]
    scale = 1 + sum(portions) // (1 << 30)
    return np.cumsum(np.array([max(1, weight // scale) for weight in portions]))


def ranked(key, extent, amount, skew):
    listing = rank_bounds(amount, skew)
    lot = jax.random.randint(jax.random.fold_in(key, 1), extent, 0, int(listing[amount - 1]))
    rank = jnp.searchsorted(jnp.asarray(listing, jnp.int32), lot, side="right")
    return jax.random.permutation(jax.random.fold_in(key, 2), amount)[rank].astype(jnp.int32)


def profile(count, total, reach, slope):
    portions = [(1 << 20) // math.isqrt(rank ** slope) + 1 for rank in range(2, count + 1)]
    spare, counts = total - reach - (count - 1), [1] * (count - 1)
    while spare > 0:
        candidates = [i for i in range(count - 1) if counts[i] < reach]
        mass, budget = sum([portions[i] for i in candidates]), spare
        for i in candidates:
            more = min(reach - counts[i], max(1, budget * portions[i] // mass), spare)
            counts[i] = counts[i] + more
            spare = spare - more
    return np.array([reach] + counts)


def uneven(own_key, amount, total, reach, lean):
    if amount == 2:
        one = jax.random.randint(own_key, (), max(1, total - reach), min(reach, total - 1) + 1)
        return jnp.stack([one, total - one])
    tallies = jnp.asarray(profile(amount, total, reach, lean), jnp.int32)
    couples = (amount - 1) // 2
    donor, receiver = tallies[1:1 + 2 * couples:2], tallies[2:2 + 2 * couples:2]
    room = jnp.minimum(donor - 1, reach - receiver)
    moved = jax.random.randint(jax.random.fold_in(own_key, 1), (couples,), 0, 1 << 20) % (room + 1)
    tallies = tallies.at[1:1 + 2 * couples:2].set(donor - moved).at[2:2 + 2 * couples:2].set(receiver + moved)
    return tallies[jax.random.permutation(jax.random.fold_in(own_key, 2), amount)]


def noise(rng, dims, spread, limit, cuts=(), kind=jnp.bfloat16):
    result = jax.random.normal(rng, dims, jnp.float32) * spread
    if len(cuts) > 0:
        result = block_scale(rng, dims, cuts, -0.22, 0.18) * result
    return jnp.clip(result, min=-limit, max=limit).astype(kind)


def setup_inputs(seed: int = 0) -> dict:
    key_list = jax.random.split(jax.random.key(seed), 9)
    return {
        "queries": noise(key_list[0], (ROWS, HEADS * HDIM), 1.0, 6.0, ((0, 256),)),
        "key_rows": noise(key_list[1], (ROWS, HEADS * HDIM), 1.0, 6.0, ((0, 256),)),
        "value_rows": noise(key_list[2], (ROWS, HEADS * HDIM), 1.0, 6.0, ((0, 256),)),
        "slopes": jnp.clip(jnp.exp(jax.random.uniform(key_list[3], (HEADS,), jnp.float32, math.log(0.002), math.log(0.1))), 0.002, 0.1),
        "norm_gain": jnp.clip(1.0 + 0.1 * jax.random.normal(key_list[4], (HEADS * HDIM,), jnp.float32), 0.5, 1.5),
        "parents": place_ends(ranked(key_list[5], (CH,), PARENTS, 2), jax.random.fold_in(key_list[5], 3), 0, PARENTS - 1).astype(jnp.int32),
        "lengths": uneven(key_list[6], CH, CH * SEG // 2, SEG, 2).astype(jnp.int32),
        "parent_states": noise(key_list[7], (PARENTS, HEADS, HDIM, HDIM), 16.0, 96.0, ((0, 16), (1, 16)), jnp.float32),
    }


EPS = 1e-06
HIGHEST = lax.Precision.HIGHEST

def lightning(query, key_part, value_part, start, lens, slopes):
    length_seg = query.shape[1]
    places = jnp.arange(length_seg, dtype=jnp.float32)
    offset = places[:, None] - places[None, :]
    decays = jnp.where(offset[None] >= 0.0, jnp.exp(-slopes[:, None, None] * jnp.maximum(offset, 0.0)[None]), 0.0)
    query_f = query.astype(jnp.float32)
    key_f = key_part.astype(jnp.float32)
    value_f = value_part.astype(jnp.float32)
    scores = jnp.einsum('cthe,cshe->chts', query_f, key_f, precision=HIGHEST)
    weights = (scores * decays[None]).astype(jnp.bfloat16).astype(jnp.float32)
    within = jnp.einsum('chts,cshe->cthe', weights, value_f, precision=HIGHEST)
    leading = jnp.exp(-slopes[None, :] * (places[:, None] + 1.0))
    scaled = query_f * leading[None, :, :, None]
    carried = jnp.einsum('cthe,chef->cthf', scaled, start, precision=HIGHEST)
    lens_f = lens.astype(jnp.float32)
    active = (places[None, :] < lens_f[:, None]).astype(jnp.float32)
    attended = ((within + carried) * active[:, :, None, None]).astype(jnp.bfloat16)
    remain = lens_f[:, None] - 1.0 - places[None, :]
    trailing = jnp.where(remain[:, :, None] >= 0.0, jnp.exp(-slopes[None, None, :] * jnp.maximum(remain, 0.0)[:, :, None]), 0.0)
    weighted_keys = key_f * trailing[..., None]
    update = jnp.einsum('cshe,cshf->chef', weighted_keys, value_f, precision=HIGHEST)
    fading = jnp.exp(-slopes[None, :] * lens_f[:, None])
    states = fading[:, :, None, None] * start + update
    return (attended, states)

def reference(queries, key_rows, value_rows, slopes, norm_gain, parents, lengths, parent_states):
    query_all = queries.reshape(CH, SEG, HEADS, HDIM)
    key_all = key_rows.reshape(CH, SEG, HEADS, HDIM)
    value_all = value_rows.reshape(CH, SEG, HEADS, HDIM)

    def per_child(items):
        start = lax.dynamic_index_in_dim(parent_states, items[3].astype(jnp.int32), 0, keepdims=True)
        attended, new_state = lightning(items[0][None], items[1][None], items[2][None], start, items[4][None], slopes)
        return (attended[0], new_state[0])
    attended, child_states = lax.map(per_child, (query_all, key_all, value_all, parents, lengths))
    rows_flat = attended.reshape(CH * SEG, HEADS * HDIM).astype(jnp.float32)
    square_mean = lax.optimization_barrier(jnp.mean(rows_flat * rows_flat, axis=-1, keepdims=True))
    mixed = (rows_flat * lax.rsqrt(square_mean + EPS) * norm_gain).astype(jnp.bfloat16)
    return (mixed, child_states)
```

```python
import jax
import jax.numpy as jnp
from jax import lax
from jax.experimental import pallas as pl
from jax.experimental.pallas import tpu as pltpu
from jax.sharding import PartitionSpec as P

EPS = 1e-06
MESH = pl.DeviceIdType.MESH
SIDE = 4
RING = 8
GROUP = 16
HEADS = 32
DIM = 128
SEG = 256
PAIR = 2 * DIM
CUTS = 4
FAR = 1e9


def ring_step(i):
    j = i // 2
    off = RING // 2 + ((j + 1) // 2) * (1 - 2 * (j % 2))
    return off, (i + 1) % 2


def exchange(
    q_hbm, k_hbm, v_hbm, slopes, parents, lengths, states,
    att_hbm, got_u, start_hbm,
    q, k, v, total, att, offsets, sent_u, bank, picked, got_s,
    load_sem, bank_send, bank_hop, bank_recv, u_send, u_recv, s_send, s_recv, out_sem, own_sem,
):
    me_d = lax.axis_index("dp")
    me_e = lax.axis_index("expert")
    y, x = me_d // SIDE, me_d % SIDE
    z, core = me_e // 2, me_e % 2

    arrays = ((k_hbm, k), (v_hbm, v), (q_hbm, q))

    def load(n, cut):
        rows = pl.ds(cut * (SEG // CUTS), SEG // CUTS)
        src, dst = arrays[n]
        return pltpu.make_async_copy(src.at[rows], dst.at[rows], load_sem.at[n, cut])

    for n in range(3):
        for cut in range(CUTS):
            load(n, cut).start()

    def along(head, j):
        return y * SIDE + (x + j) % SIDE if head == 0 else ((y + j) % SIDE) * SIDE + x

    barrier = pltpu.get_barrier_semaphore()

    def greet(i, _):
        pl.semaphore_signal(
            barrier, inc=1, device_id=(me_d, (me_e + i) % GROUP), device_id_type=MESH
        )
        return 0

    lax.fori_loop(1, GROUP, greet, 0)
    for head in range(2):
        for j in range(1, SIDE):
            pl.semaphore_signal(
                barrier, inc=1, device_id=(along(head, j), me_e), device_id_type=MESH
            )

    for head in range(2):
        for parent in range(2):
            bank[head, 2 * me_d + parent] = states[parent, head].astype(jnp.bfloat16)

    t_of = lax.broadcasted_iota(jnp.int32, (SEG, SEG), 0)
    s_of = lax.broadcasted_iota(jnp.int32, (SEG, SEG), 1)
    offsets[...] = jnp.where(t_of >= s_of, (t_of - s_of).astype(jnp.float32), FAR)

    length = lengths[me_e]
    place = lax.broadcasted_iota(jnp.int32, (SEG, DIM), 0)
    remain = (length - 1 - place).astype(jnp.float32)
    inside = place < length
    step_of = (place + 1).astype(jnp.float32)

    pl.semaphore_wait(barrier, GROUP - 1 + 2 * (SIDE - 1))

    def block(head, d):
        return bank.at[head, pl.ds(2 * d, 2)]

    def bank_copy(head, d, to, sem):
        return pltpu.make_async_remote_copy(
            src_ref=block(head, d), dst_ref=block(head, d), send_sem=sem,
            recv_sem=bank_recv.at[head, d], device_id=(to, me_e), device_id_type=MESH,
        )

    def first_hop(head, j):
        return bank_copy(head, me_d, along(head, j), bank_send.at[head, j - 1])

    def second_hop(head, b, j):
        return bank_copy(head, along(head, b), along(1 - head, j), bank_hop.at[head, b, j - 1])

    for head in range(2):
        for j in range(1, SIDE):
            first_hop(head, j).start()
    for head in range(2):
        for j in range(1, SIDE):
            second_hop(head, 0, j).start()

    for cut in range(CUTS):
        load(0, cut).wait()
        load(1, cut).wait()

    def columns(e):
        return pl.ds(pl.multiple_of(e * PAIR, PAIR), PAIR)

    def head_columns(e, head):
        return pl.ds(pl.multiple_of(e * PAIR + head * DIM, DIM), DIM)

    def partner(i):
        off, flip = ring_step(i)
        return 2 * ((z + off) % RING) + (core + flip) % 2

    def source(i):
        off, flip = ring_step(i)
        return 2 * ((z + RING - off) % RING) + (core + flip) % 2

    def send_u(e):
        return pltpu.make_async_remote_copy(
            src_ref=sent_u.at[e], dst_ref=got_u.at[me_e], send_sem=u_send.at[e],
            recv_sem=u_recv.at[me_e], device_id=(me_d, e), device_id_type=MESH,
        )

    def recv_u(e):
        return pltpu.make_async_remote_copy(
            src_ref=sent_u.at[e], dst_ref=got_u.at[e], send_sem=u_send.at[e],
            recv_sem=u_recv.at[e], device_id=(me_d, e), device_id_type=MESH,
        )

    def send_s(e):
        return pltpu.make_async_remote_copy(
            src_ref=picked.at[e], dst_ref=got_s.at[me_e], send_sem=s_send.at[e],
            recv_sem=s_recv.at[me_e], device_id=(me_d, e), device_id_type=MESH,
        )

    def recv_s(e):
        return pltpu.make_async_remote_copy(
            src_ref=picked.at[e], dst_ref=got_s.at[e], send_sem=s_send.at[e],
            recv_sem=s_recv.at[e], device_id=(me_d, e), device_id_type=MESH,
        )

    def update(e):
        for head in range(2):
            cols = head_columns(e, head)
            slope = slopes[2 * e + head]
            fade = jnp.where(remain >= 0.0, jnp.exp(-slope * jnp.maximum(remain, 0.0)), 0.0)
            keys = (k[:, cols].astype(jnp.float32) * fade).astype(jnp.bfloat16)
            sent_u[e, head] = lax.dot_general(
                keys, v[:, cols], (((0,), (0,)), ((), ())), preferred_element_type=jnp.float32
            ).astype(jnp.bfloat16)

    def update_step(i, _):
        e = partner(i)
        update(e)
        send_u(e).start()
        return 0

    lax.fori_loop(0, GROUP - 1, update_step, 0)
    update(me_e)
    own_u = pltpu.make_async_copy(sent_u.at[me_e], got_u.at[me_e], own_sem.at[0])
    own_u.start()

    for b in range(1, SIDE):
        for head in range(2):
            d = along(head, b)
            bank_copy(head, d, d, bank_send.at[head, 0]).wait_recv()
            for j in range(1, SIDE):
                second_hop(head, b, j).start()

    for cut in range(CUTS):
        load(2, cut).wait()

    def within(i, _):
        cols = pl.ds(pl.multiple_of(i * DIM, DIM), DIM)
        decay = jnp.exp(-slopes[i] * offsets[...])
        scores = lax.dot_general(
            q[:, cols], k[:, cols], (((1,), (1,)), ((), ())), preferred_element_type=jnp.float32
        )
        total[:, cols] = jnp.dot(
            (scores * decay).astype(jnp.bfloat16), v[:, cols], preferred_element_type=jnp.float32
        )
        return 0

    lax.fori_loop(0, HEADS, within, 0)

    for j in range(1, SIDE):
        for b in range(SIDE):
            d = ((y + j) % SIDE) * SIDE + (x + b) % SIDE
            bank_copy(0, d, along(0, 1), bank_send.at[0, 0]).wait_recv()
            d = ((y + b) % SIDE) * SIDE + (x + j) % SIDE
            bank_copy(1, d, along(0, 1), bank_send.at[0, 0]).wait_recv()

    def pick(e):
        parent = parents[e]
        for head in range(2):
            picked[e, head] = bank[head, parent]

    def pick_step(i, _):
        e = partner(i)
        pick(e)
        send_s(e).start()
        return 0

    lax.fori_loop(0, GROUP - 1, pick_step, 0)
    pick(me_e)
    keep = pltpu.make_async_copy(picked, start_hbm, own_sem.at[1])
    keep.start()

    def att_out(e):
        return pltpu.make_async_copy(att.at[:, columns(e)], att_hbm.at[:, columns(e)], out_sem.at[e])

    def finish(e, src, at):
        for head in range(2):
            cols = head_columns(e, head)
            lead = jnp.exp(-slopes[2 * e + head] * step_of)
            carried = jnp.dot(q[:, cols], src[at, head], preferred_element_type=jnp.float32)
            att[:, cols] = jnp.where(inside, total[:, cols] + carried * lead, 0.0).astype(jnp.bfloat16)
        att_out(e).start()

    finish(me_e, picked, me_e)

    def finish_step(i, _):
        e = source(i)
        recv_s(e).wait_recv()
        finish(e, got_s, e)
        return 0

    lax.fori_loop(0, GROUP - 1, finish_step, 0)

    def drain(i, _):
        e = source(i)
        recv_u(e).wait_recv()
        send_u(e).wait_send()
        send_s(e).wait_send()
        att_out(e).wait()
        return 0

    lax.fori_loop(0, GROUP - 1, drain, 0)
    att_out(me_e).wait()
    own_u.wait()
    keep.wait()
    for head in range(2):
        for j in range(1, SIDE):
            first_hop(head, j).wait_send()
            for b in range(SIDE):
                second_hop(head, b, j).wait_send()


STEPS = 8
TOKENS = SEG // STEPS
KIDS = GROUP // STEPS


def settle(att, got_u, start, slopes, lengths, gain, mixed, child):
    me_e = lax.axis_index("expert")
    at = pl.program_id(0)
    rows = att[...].astype(jnp.float32)
    mean = jnp.mean(rows * rows, axis=-1, keepdims=True)
    mixed[...] = (rows * lax.rsqrt(mean + EPS) * gain[...]).astype(jnp.bfloat16)
    for kid in range(KIDS):
        length = lengths[at * KIDS + kid].astype(jnp.float32)
        for head in range(2):
            slope = slopes[2 * me_e + head]
            fade = jnp.exp(jnp.full((DIM, DIM), -slope * length, jnp.float32))
            child[kid, head] = fade * start[kid, head].astype(jnp.float32) + got_u[
                kid, head
            ].astype(jnp.float32)


def body(queries, key_rows, value_rows, slopes, norm_gain, parents, lengths, parent_states):
    anywhere = pl.BlockSpec(memory_space=pl.ANY)
    smem = pl.BlockSpec(memory_space=pltpu.SMEM)
    vmem = pl.BlockSpec(memory_space=pltpu.VMEM)
    dma = pltpu.SemaphoreType.DMA
    bf16, f32 = jnp.bfloat16, jnp.float32
    width = HEADS * DIM
    moved = (GROUP, 2, DIM, DIM)
    att, got_u, start = pl.pallas_call(
        exchange,
        out_shape=(
            jax.ShapeDtypeStruct((SEG, width), bf16),
            jax.ShapeDtypeStruct(moved, bf16),
            jax.ShapeDtypeStruct(moved, bf16),
        ),
        in_specs=[anywhere] * 3 + [smem] * 3 + [vmem],
        out_specs=(anywhere,) * 3,
        scratch_shapes=[
            pltpu.VMEM((SEG, width), bf16),
            pltpu.VMEM((SEG, width), bf16),
            pltpu.VMEM((SEG, width), bf16),
            pltpu.VMEM((SEG, width), f32),
            pltpu.VMEM((SEG, width), bf16),
            pltpu.VMEM((SEG, SEG), f32),
            pltpu.VMEM(moved, bf16),
            pltpu.VMEM((2, 2 * SIDE * SIDE, DIM, DIM), bf16),
            pltpu.VMEM(moved, bf16),
            pltpu.VMEM(moved, bf16),
            dma((3, CUTS)),
            dma((2, SIDE - 1)),
            dma((2, SIDE, SIDE - 1)),
            dma((2, SIDE * SIDE)),
            dma((GROUP,)),
            dma((GROUP,)),
            dma((GROUP,)),
            dma((GROUP,)),
            dma((GROUP,)),
            dma((2,)),
        ],
        compiler_params=pltpu.CompilerParams(
            collective_id=0, has_side_effects=True, vmem_limit_bytes=40 * 1024 * 1024
        ),
        name="exchange",
    )(queries, key_rows, value_rows, slopes, parents, lengths, parent_states)
    mixed, child = pl.pallas_call(
        settle,
        grid=(STEPS,),
        out_shape=(
            jax.ShapeDtypeStruct((SEG, width), bf16),
            jax.ShapeDtypeStruct(moved, f32),
        ),
        in_specs=[
            pl.BlockSpec((TOKENS, width), lambda i: (i, 0)),
            pl.BlockSpec((KIDS, 2, DIM, DIM), lambda i: (i, 0, 0, 0)),
            pl.BlockSpec((KIDS, 2, DIM, DIM), lambda i: (i, 0, 0, 0)),
            smem,
            smem,
            pl.BlockSpec((1, width), lambda i: (0, 0)),
        ],
        out_specs=(
            pl.BlockSpec((TOKENS, width), lambda i: (i, 0)),
            pl.BlockSpec((KIDS, 2, DIM, DIM), lambda i: (i, 0, 0, 0)),
        ),
        compiler_params=pltpu.CompilerParams(vmem_limit_bytes=32 * 1024 * 1024),
        name="settle",
    )(att, got_u, start, slopes, lengths, norm_gain.reshape(1, width))
    return mixed, child


def solution(mesh):
    in_specs = (
        P(("dp", "expert"), None),
        P(("dp", "expert"), None),
        P(("dp", "expert"), None),
        P(),
        P(),
        P("dp"),
        P("dp"),
        P("dp", "expert", None, None),
    )
    out_specs = (P(("dp", "expert"), None), P("dp", "expert", None, None))
    return jax.shard_map(body, mesh=mesh, in_specs=in_specs, out_specs=out_specs, check_vma=False)
```

```python
import jax
import jax.numpy as jnp
from jax import lax
from jax.experimental import pallas as pl
from jax.experimental.pallas import tpu as pltpu
from jax.sharding import PartitionSpec as P

EPS = 1e-06
MESH = pl.DeviceIdType.MESH
SIDE = 4
RING = 8
GROUP = 16
HEADS = 32
DIM = 128
SEG = 256
PAIR = 2 * DIM
CUTS = 4
FAR = 1e9


def ring_step(i):
    j = i // 2
    off = RING // 2 + ((j + 1) // 2) * (1 - 2 * (j % 2))
    return off, (i + 1) % 2


def exchange(
    q_hbm, k_hbm, v_hbm, slopes_hbm, parents_hbm, lengths_hbm, states_hbm,
    att, got_u, picked,
    q, k, v, slopes, parents, lengths, states, total, offsets, sent_u, bank, got_s,
    load_sem, small_sem, bank_send, bank_hop, bank_recv, u_send, u_recv, s_send, s_recv, own_sem,
):
    me_d = lax.axis_index("dp")
    me_e = lax.axis_index("expert")
    y, x = me_d // SIDE, me_d % SIDE
    z, core = me_e // 2, me_e % 2

    arrays = ((k_hbm, k), (v_hbm, v), (q_hbm, q))

    def load(n, cut):
        rows = pl.ds(cut * (SEG // CUTS), SEG // CUTS)
        src, dst = arrays[n]
        return pltpu.make_async_copy(src.at[rows], dst.at[rows], load_sem.at[n, cut])

    smalls = [
        pltpu.make_async_copy(src, dst, small_sem.at[n])
        for n, (src, dst) in enumerate(
            ((states_hbm, states), (slopes_hbm, slopes), (lengths_hbm, lengths), (parents_hbm, parents))
        )
    ]
    for small in smalls:
        small.start()
    for n in range(3):
        for cut in range(CUTS):
            load(n, cut).start()

    def along(head, j):
        return y * SIDE + (x + j) % SIDE if head == 0 else ((y + j) % SIDE) * SIDE + x

    barrier = pltpu.get_barrier_semaphore()

    def greet(i, _):
        pl.semaphore_signal(
            barrier, inc=1, device_id=(me_d, (me_e + i) % GROUP), device_id_type=MESH
        )
        return 0

    lax.fori_loop(1, GROUP, greet, 0)
    for head in range(2):
        for j in range(1, SIDE):
            pl.semaphore_signal(
                barrier, inc=1, device_id=(along(head, j), me_e), device_id_type=MESH
            )

    for small in smalls:
        small.wait()

    for head in range(2):
        for parent in range(2):
            bank[head, 2 * me_d + parent] = states[parent, head].astype(jnp.bfloat16)

    t_of = lax.broadcasted_iota(jnp.int32, (SEG, SEG), 0)
    s_of = lax.broadcasted_iota(jnp.int32, (SEG, SEG), 1)
    offsets[...] = jnp.where(t_of >= s_of, (t_of - s_of).astype(jnp.float32), FAR)

    length = lengths[me_e]
    place = lax.broadcasted_iota(jnp.int32, (SEG, DIM), 0)
    remain = (length - 1 - place).astype(jnp.float32)
    inside = place < length
    step_of = (place + 1).astype(jnp.float32)

    def head_columns(e, head):
        return pl.ds(pl.multiple_of(e * PAIR + head * DIM, DIM), DIM)

    def partner(i):
        off, flip = ring_step(i)
        return 2 * ((z + off) % RING) + (core + flip) % 2

    def source(i):
        off, flip = ring_step(i)
        return 2 * ((z + RING - off) % RING) + (core + flip) % 2

    def update(e):
        for head in range(2):
            cols = head_columns(e, head)
            slope = slopes[2 * e + head]
            fade = jnp.where(remain >= 0.0, jnp.exp(-slope * jnp.maximum(remain, 0.0)), 0.0)
            keys = (k[:, cols].astype(jnp.float32) * fade).astype(jnp.bfloat16)
            sent_u[e, head] = lax.dot_general(
                keys, v[:, cols], (((0,), (0,)), ((), ())), preferred_element_type=jnp.float32
            ).astype(jnp.bfloat16)

    for cut in range(CUTS):
        load(0, cut).wait()
        load(1, cut).wait()
    update(partner(0))

    pl.semaphore_wait(barrier, GROUP - 1 + 2 * (SIDE - 1))

    def block(head, d):
        return bank.at[head, pl.ds(2 * d, 2)]

    def bank_copy(head, d, to, sem):
        return pltpu.make_async_remote_copy(
            src_ref=block(head, d), dst_ref=block(head, d), send_sem=sem,
            recv_sem=bank_recv.at[head, d], device_id=(to, me_e), device_id_type=MESH,
        )

    def first_hop(head, j):
        return bank_copy(head, me_d, along(head, j), bank_send.at[head, j - 1])

    def second_hop(head, b, j):
        return bank_copy(head, along(head, b), along(1 - head, j), bank_hop.at[head, b, j - 1])

    for head in range(2):
        for j in range(1, SIDE):
            first_hop(head, j).start()
    for head in range(2):
        for j in range(1, SIDE):
            second_hop(head, 0, j).start()

    def send_u(e):
        return pltpu.make_async_remote_copy(
            src_ref=sent_u.at[e], dst_ref=got_u.at[me_e], send_sem=u_send.at[e],
            recv_sem=u_recv.at[me_e], device_id=(me_d, e), device_id_type=MESH,
        )

    def recv_u(e):
        return pltpu.make_async_remote_copy(
            src_ref=sent_u.at[e], dst_ref=got_u.at[e], send_sem=u_send.at[e],
            recv_sem=u_recv.at[e], device_id=(me_d, e), device_id_type=MESH,
        )

    def send_s(e):
        return pltpu.make_async_remote_copy(
            src_ref=picked.at[e], dst_ref=got_s.at[me_e], send_sem=s_send.at[e],
            recv_sem=s_recv.at[me_e], device_id=(me_d, e), device_id_type=MESH,
        )

    def recv_s(e):
        return pltpu.make_async_remote_copy(
            src_ref=picked.at[e], dst_ref=got_s.at[e], send_sem=s_send.at[e],
            recv_sem=s_recv.at[e], device_id=(me_d, e), device_id_type=MESH,
        )

    def update_step(i, _):
        send_u(partner(i)).start()
        update(partner(i + 1))
        return 0

    lax.fori_loop(0, GROUP - 1, update_step, 0)
    own_u = pltpu.make_async_copy(sent_u.at[me_e], got_u.at[me_e], own_sem.at[0])
    own_u.start()

    for b in range(1, SIDE):
        for head in range(2):
            d = along(head, b)
            bank_copy(head, d, d, bank_send.at[head, 0]).wait_recv()
            for j in range(1, SIDE):
                second_hop(head, b, j).start()

    for cut in range(CUTS):
        load(2, cut).wait()

    def within(i, _):
        cols = pl.ds(pl.multiple_of(i * DIM, DIM), DIM)
        decay = jnp.exp(-slopes[i] * offsets[...])
        scores = lax.dot_general(
            q[:, cols], k[:, cols], (((1,), (1,)), ((), ())), preferred_element_type=jnp.float32
        )
        total[:, cols] = jnp.dot(
            (scores * decay).astype(jnp.bfloat16), v[:, cols], preferred_element_type=jnp.float32
        )
        return 0

    lax.fori_loop(0, HEADS, within, 0)

    for j in range(1, SIDE):
        for b in range(SIDE):
            d = ((y + j) % SIDE) * SIDE + (x + b) % SIDE
            bank_copy(0, d, along(0, 1), bank_send.at[0, 0]).wait_recv()
            d = ((y + b) % SIDE) * SIDE + (x + j) % SIDE
            bank_copy(1, d, along(0, 1), bank_send.at[0, 0]).wait_recv()

    def pick(e):
        parent = parents[e]
        for head in range(2):
            picked[e, head] = bank[head, parent]

    def pick_step(i, _):
        e = partner(i)
        pick(e)
        send_s(e).start()
        return 0

    lax.fori_loop(0, GROUP - 1, pick_step, 0)
    pick(me_e)

    def finish(e, src, at):
        for head in range(2):
            cols = head_columns(e, head)
            lead = jnp.exp(-slopes[2 * e + head] * step_of)
            carried = jnp.dot(q[:, cols], src[at, head], preferred_element_type=jnp.float32)
            att[:, cols] = jnp.where(inside, total[:, cols] + carried * lead, 0.0).astype(jnp.bfloat16)

    finish(me_e, picked, me_e)

    def finish_step(i, _):
        e = source(i)
        recv_s(e).wait_recv()
        finish(e, got_s, e)
        return 0

    lax.fori_loop(0, GROUP - 1, finish_step, 0)

    def drain(i, _):
        e = source(i)
        recv_u(e).wait_recv()
        send_u(e).wait_send()
        send_s(e).wait_send()
        return 0

    lax.fori_loop(0, GROUP - 1, drain, 0)
    own_u.wait()
    for head in range(2):
        for j in range(1, SIDE):
            first_hop(head, j).wait_send()
            for b in range(SIDE):
                second_hop(head, b, j).wait_send()


STEPS = 8
TOKENS = SEG // STEPS
KIDS = GROUP // STEPS


def settle(att, got_u, start, gain, slopes, lengths, mixed_hbm, child_hbm, mixed, child, sem):
    me_e = lax.axis_index("expert")

    def out(at):
        rows, kids = pl.ds(at * TOKENS, TOKENS), pl.ds(at * KIDS, KIDS)
        return (
            pltpu.make_async_copy(mixed.at[rows], mixed_hbm.at[rows], sem.at[0, at]),
            pltpu.make_async_copy(child.at[kids], child_hbm.at[kids], sem.at[1, at]),
        )

    def step(at, _):
        for kid in range(KIDS):
            length = lengths[at * KIDS + kid].astype(jnp.float32)
            for head in range(2):
                slope = slopes[2 * me_e + head]
                fade = jnp.exp(jnp.full((1, DIM), -slope * length, jnp.float32))
                child[at * KIDS + kid, head] = fade * start[at * KIDS + kid, head].astype(
                    jnp.float32
                ) + got_u[at * KIDS + kid, head].astype(jnp.float32)
        out(at)[1].start()
        here = pl.ds(pl.multiple_of(at * TOKENS, TOKENS), TOKENS)
        rows = att[here, :].astype(jnp.float32)
        mean = jnp.mean(rows * rows, axis=-1, keepdims=True)
        mixed[here, :] = (rows * lax.rsqrt(mean + EPS) * gain[...]).astype(jnp.bfloat16)
        out(at)[0].start()
        return 0

    lax.fori_loop(0, STEPS, step, 0)
    for at in range(STEPS):
        for copy in out(at):
            copy.wait()


def body(queries, key_rows, value_rows, slopes, norm_gain, parents, lengths, parent_states):
    anywhere = pl.BlockSpec(memory_space=pl.ANY)
    smem = pl.BlockSpec(memory_space=pltpu.SMEM)
    vmem = pl.BlockSpec(memory_space=pltpu.VMEM)
    dma = pltpu.SemaphoreType.DMA
    bf16, f32 = jnp.bfloat16, jnp.float32
    width = HEADS * DIM
    moved = (GROUP, 2, DIM, DIM)
    in_hbm = [
        pltpu.with_memory_space_constraint(a, pltpu.HBM)
        for a in (queries, key_rows, value_rows, slopes, parents, lengths, parent_states)
    ]
    att, got_u, start = pl.pallas_call(
        exchange,
        out_shape=(
            jax.ShapeDtypeStruct((SEG, width), bf16),
            jax.ShapeDtypeStruct(moved, bf16),
            jax.ShapeDtypeStruct(moved, bf16),
        ),
        in_specs=[anywhere] * 7,
        out_specs=(vmem,) * 3,
        scratch_shapes=[
            pltpu.VMEM((SEG, width), bf16),
            pltpu.VMEM((SEG, width), bf16),
            pltpu.VMEM((SEG, width), bf16),
            pltpu.SMEM((HEADS,), f32),
            pltpu.SMEM((GROUP,), jnp.int32),
            pltpu.SMEM((GROUP,), jnp.int32),
            pltpu.VMEM((2, 2, DIM, DIM), f32),
            pltpu.VMEM((SEG, width), f32),
            pltpu.VMEM((SEG, SEG), f32),
            pltpu.VMEM(moved, bf16),
            pltpu.VMEM((2, 2 * SIDE * SIDE, DIM, DIM), bf16),
            pltpu.VMEM(moved, bf16),
            dma((3, CUTS)),
            dma((4,)),
            dma((2, SIDE - 1)),
            dma((2, SIDE, SIDE - 1)),
            dma((2, SIDE * SIDE)),
            dma((GROUP,)),
            dma((GROUP,)),
            dma((GROUP,)),
            dma((GROUP,)),
            dma((1,)),
        ],
        compiler_params=pltpu.CompilerParams(
            collective_id=0, has_side_effects=True, vmem_limit_bytes=40 * 1024 * 1024
        ),
        name="exchange",
    )(*in_hbm)
    mixed, child = pl.pallas_call(
        settle,
        out_shape=(
            jax.ShapeDtypeStruct((SEG, width), bf16),
            jax.ShapeDtypeStruct(moved, f32),
        ),
        in_specs=[vmem] * 4 + [smem] * 2,
        out_specs=(anywhere,) * 2,
        scratch_shapes=[
            pltpu.VMEM((SEG, width), bf16),
            pltpu.VMEM(moved, f32),
            dma((2, STEPS)),
        ],
        compiler_params=pltpu.CompilerParams(vmem_limit_bytes=40 * 1024 * 1024),
        name="settle",
    )(att, got_u, start, norm_gain.reshape(1, width), slopes, lengths)
    return mixed, child


def solution(mesh):
    in_specs = (
        P(("dp", "expert"), None),
        P(("dp", "expert"), None),
        P(("dp", "expert"), None),
        P(),
        P(),
        P("dp"),
        P("dp"),
        P("dp", "expert", None, None),
    )
    out_specs = (P(("dp", "expert"), None), P("dp", "expert", None, None))
    return jax.shard_map(body, mesh=mesh, in_specs=in_specs, out_specs=out_specs, check_vma=False)
```

```python
import jax
import jax.numpy as jnp
from jax import lax
from jax.experimental import pallas as pl
from jax.experimental.pallas import tpu as pltpu
from jax.sharding import PartitionSpec as P

EPS = 1e-06
MESH = pl.DeviceIdType.MESH
SIDE = 4
RING = 8
GROUP = 16
HEADS = 32
DIM = 128
SEG = 256
PAIR = 2 * DIM
CUTS = 4
FAR = 1e9
EARLY, MIDDLE = 10, 22


def ring_step(i):
    j = i // 2
    off = RING // 2 + ((j + 1) // 2) * (1 - 2 * (j % 2))
    return off, (i + 1) % 2


def exchange(
    q_hbm, k_hbm, v_hbm, slopes_hbm, parents_hbm, lengths_hbm, states_hbm,
    att, child,
    q, k, v, slopes, parents, lengths, states, total, offsets, sent_u, got_u, bank_own, bank_far, picked, passed, got_s,
    load_sem, small_sem, swap_sem, bank_send, bank_hop, bank_recv, u_send, u_recv, s_send, p_send, s_recv,
):
    me_d = lax.axis_index("dp")
    me_e = lax.axis_index("expert")
    y, x = me_d // SIDE, me_d % SIDE
    z, core = me_e // 2, me_e % 2
    across = (me_e + GROUP // 2) % GROUP

    arrays = ((k_hbm, k), (v_hbm, v), (q_hbm, q))

    def load(n, cut):
        rows = pl.ds(cut * (SEG // CUTS), SEG // CUTS)
        src, dst = arrays[n]
        return pltpu.make_async_copy(src.at[rows], dst.at[rows], load_sem.at[n, cut])

    smalls = [
        pltpu.make_async_copy(src, dst, small_sem.at[n])
        for n, (src, dst) in enumerate(
            ((states_hbm, states), (slopes_hbm, slopes), (lengths_hbm, lengths), (parents_hbm, parents))
        )
    ]
    for small in smalls:
        small.start()
    for n in range(3):
        for cut in range(CUTS):
            load(n, cut).start()

    def along(slot, j):
        return y * SIDE + (x + j) % SIDE if slot % 2 == 0 else ((y + j) % SIDE) * SIDE + x

    barrier = pltpu.get_barrier_semaphore()

    def greet(i, _):
        pl.semaphore_signal(
            barrier, inc=1, device_id=(me_d, (me_e + i) % GROUP), device_id_type=MESH
        )
        return 0

    lax.fori_loop(1, GROUP, greet, 0)
    for slot in range(2):
        for j in range(1, SIDE):
            pl.semaphore_signal(
                barrier, inc=1, device_id=(along(slot, j), me_e), device_id_type=MESH
            )

    for small in smalls:
        small.wait()

    for slot in range(2):
        for parent in range(2):
            bank_own[slot, 2 * me_d + parent] = states[parent, slot].astype(jnp.bfloat16)

    t_of = lax.broadcasted_iota(jnp.int32, (SEG, SEG), 0)
    s_of = lax.broadcasted_iota(jnp.int32, (SEG, SEG), 1)
    offsets[...] = jnp.where(t_of >= s_of, (t_of - s_of).astype(jnp.float32), FAR)

    length = lengths[me_e]
    place = lax.broadcasted_iota(jnp.int32, (SEG, DIM), 0)
    remain = (length - 1 - place).astype(jnp.float32)
    inside = place < length
    step_of = (place + 1).astype(jnp.float32)

    def head_columns(e, head):
        return pl.ds(pl.multiple_of(e * PAIR + head * DIM, DIM), DIM)

    def device(off, flip):
        return 2 * ((z + off) % RING) + (core + flip) % 2

    def partner(i):
        return device(*ring_step(i))

    def source(i):
        off, flip = ring_step(i)
        return device(RING - off, flip)

    def near(far, i):
        return device(far + (RING - 2 * far) * (i // 2), i % 2)

    other = device(0, 1)

    def update(e):
        for head in range(2):
            cols = head_columns(e, head)
            slope = slopes[2 * e + head]
            fade = jnp.where(remain >= 0.0, jnp.exp(-slope * jnp.maximum(remain, 0.0)), 0.0)
            keys = (k[:, cols].astype(jnp.float32) * fade).astype(jnp.bfloat16)
            sent_u[e, head] = lax.dot_general(
                keys, v[:, cols], (((0,), (0,)), ((), ())), preferred_element_type=jnp.float32
            ).astype(jnp.bfloat16)

    for cut in range(CUTS):
        load(0, cut).wait()
        load(1, cut).wait()
    update(partner(0))

    pl.semaphore_wait(barrier, GROUP - 1 + 2 * (SIDE - 1))

    swap = pltpu.make_async_remote_copy(
        src_ref=bank_own.at[:, pl.ds(2 * me_d, 2)],
        dst_ref=bank_far.at[:, pl.ds(2 * me_d, 2)],
        send_sem=swap_sem.at[0], recv_sem=swap_sem.at[1],
        device_id=(me_d, across), device_id_type=MESH,
    )
    swap.start()

    def bank_copy(slot, d, to, sem):
        block = (bank_own, bank_far)[slot // 2].at[slot % 2, pl.ds(2 * d, 2)]
        return pltpu.make_async_remote_copy(
            src_ref=block, dst_ref=block, send_sem=sem,
            recv_sem=bank_recv.at[slot, d], device_id=(to, me_e), device_id_type=MESH,
        )

    def first_hop(slot, j):
        return bank_copy(slot, me_d, along(slot, j), bank_send.at[slot, j - 1])

    def second_hop(slot, b, j):
        return bank_copy(slot, along(slot, b), along(slot + 1, j), bank_hop.at[slot, b, j - 1])

    def arrival(slot, d):
        bank_copy(slot, d, along(0, 1), bank_send.at[slot, 0]).wait_recv()

    def open_gather(slots):
        for slot in slots:
            for j in range(1, SIDE):
                first_hop(slot, j).start()
        for slot in slots:
            for j in range(1, SIDE):
                second_hop(slot, 0, j).start()

    def pass_on(slots):
        for b in range(1, SIDE):
            for slot in slots:
                arrival(slot, along(slot, b))
                for j in range(1, SIDE):
                    second_hop(slot, b, j).start()

    def close_gather(slots):
        for j in range(1, SIDE):
            for b in range(SIDE):
                for slot in slots:
                    if slot % 2 == 0:
                        arrival(slot, ((y + j) % SIDE) * SIDE + (x + b) % SIDE)
                    else:
                        arrival(slot, ((y + b) % SIDE) * SIDE + (x + j) % SIDE)

    open_gather((0, 1))

    def send_u(e):
        return pltpu.make_async_remote_copy(
            src_ref=sent_u.at[e], dst_ref=got_u.at[me_e], send_sem=u_send.at[e],
            recv_sem=u_recv.at[me_e], device_id=(me_d, e), device_id_type=MESH,
        )

    def recv_u(e):
        return pltpu.make_async_remote_copy(
            src_ref=sent_u.at[e], dst_ref=got_u.at[e], send_sem=u_send.at[e],
            recv_sem=u_recv.at[e], device_id=(me_d, e), device_id_type=MESH,
        )

    def send_s(e):
        return pltpu.make_async_remote_copy(
            src_ref=picked.at[e], dst_ref=got_s.at[me_e], send_sem=s_send.at[e],
            recv_sem=s_recv.at[me_e], device_id=(me_d, e), device_id_type=MESH,
        )

    def send_p(e):
        return pltpu.make_async_remote_copy(
            src_ref=passed.at[e], dst_ref=got_s.at[across], send_sem=p_send.at[e],
            recv_sem=s_recv.at[across], device_id=(me_d, e), device_id_type=MESH,
        )

    def recv_s(e):
        return pltpu.make_async_remote_copy(
            src_ref=picked.at[e], dst_ref=got_s.at[e], send_sem=s_send.at[e],
            recv_sem=s_recv.at[e], device_id=(me_d, e), device_id_type=MESH,
        )

    def update_step(i, _):
        send_u(partner(i)).start()
        update(partner(i + 1))
        return 0

    lax.fori_loop(0, GROUP - 1, update_step, 0)

    pass_on((0, 1))
    swap.wait_recv()
    open_gather((2, 3))

    for cut in range(CUTS):
        load(2, cut).wait()

    def within(i, _):
        cols = pl.ds(pl.multiple_of(i * DIM, DIM), DIM)
        decay = jnp.exp(-slopes[i] * offsets[...])
        scores = lax.dot_general(
            q[:, cols], k[:, cols], (((1,), (1,)), ((), ())), preferred_element_type=jnp.float32
        )
        total[:, cols] = jnp.dot(
            (scores * decay).astype(jnp.bfloat16), v[:, cols], preferred_element_type=jnp.float32
        )
        return 0

    lax.fori_loop(0, EARLY, within, 0)
    pass_on((2, 3))
    lax.fori_loop(EARLY, MIDDLE, within, 0)

    def pick(e, bank, into):
        parent = parents[e]
        for head in range(2):
            into[e, head] = bank[head, parent]

    def pick_far(i, _):
        e = near(2, i)
        pick(e, bank_own, picked)
        send_s(e).start()
        return 0

    def pick_next(i, _):
        e = near(1, i)
        pick(e, bank_own, picked)
        send_s(e).start()
        return 0

    def pick_rest(i, _):
        off = 3 + i // 2
        pick(device(off, i % 2), bank_own, picked)
        return 0

    close_gather((0, 1))
    lax.fori_loop(0, 4, pick_far, 0)
    lax.fori_loop(0, 4, pick_next, 0)
    pick(other, bank_own, picked)
    send_s(other).start()
    pick(me_e, bank_own, picked)
    lax.fori_loop(0, 6, pick_rest, 0)

    lax.fori_loop(MIDDLE, HEADS, within, 0)

    def grow(e, fresh):
        for head in range(2):
            fade = jnp.exp(
                jnp.full((1, DIM), -slopes[2 * me_e + head] * lengths[e].astype(jnp.float32), jnp.float32)
            )
            child[e, head] = fade * picked[e, head].astype(jnp.float32) + fresh[e, head].astype(
                jnp.float32
            )

    def grow_step(i, _):
        e = source(i)
        recv_u(e).wait_recv()
        grow(e, got_u)
        return 0

    grow(me_e, sent_u)
    lax.fori_loop(0, GROUP - 1, grow_step, 0)

    def pass_next(i, _):
        e = near(1, i)
        pick(e, bank_far, passed)
        send_p(e).start()
        return 0

    close_gather((2, 3))
    lax.fori_loop(0, 4, pass_next, 0)
    pick(other, bank_far, passed)
    send_p(other).start()
    pick(me_e, bank_far, passed)

    def finish(e, src, at):
        for head in range(2):
            cols = head_columns(e, head)
            lead = jnp.exp(-slopes[2 * e + head] * step_of)
            carried = jnp.dot(q[:, cols], src[at, head], preferred_element_type=jnp.float32)
            att[:, cols] = jnp.where(inside, total[:, cols] + carried * lead, 0.0).astype(jnp.bfloat16)

    def arrived(e):
        recv_s(e).wait_recv()
        finish(e, got_s, e)

    def finish_far(i, _):
        arrived(near(2, i))
        return 0

    def finish_next(i, _):
        arrived(near(1, i))
        return 0

    def finish_passed(i, _):
        arrived((near(1, i) + GROUP // 2) % GROUP)
        return 0

    finish(me_e, picked, me_e)
    finish(across, passed, me_e)
    arrived(other)
    lax.fori_loop(0, 4, finish_far, 0)
    lax.fori_loop(0, 4, finish_next, 0)
    arrived((other + GROUP // 2) % GROUP)
    lax.fori_loop(0, 4, finish_passed, 0)

    def drain_u(i, _):
        send_u(partner(i)).wait_send()
        return 0

    def drain_s(i, _):
        send_s(near(2, i)).wait_send()
        send_s(near(1, i)).wait_send()
        send_p(near(1, i)).wait_send()
        return 0

    lax.fori_loop(0, GROUP - 1, drain_u, 0)
    lax.fori_loop(0, 4, drain_s, 0)
    send_s(other).wait_send()
    send_p(other).wait_send()
    swap.wait_send()
    for slot in range(4):
        for j in range(1, SIDE):
            first_hop(slot, j).wait_send()
            for b in range(SIDE):
                second_hop(slot, b, j).wait_send()


STEPS = 8
TOKENS = SEG // STEPS


def settle(att, child, gain, mixed_hbm, child_hbm, mixed, child_sem, mixed_sem):
    kids = GROUP // STEPS

    def child_out(at):
        part = pl.ds(at * kids, kids)
        return pltpu.make_async_copy(child.at[part], child_hbm.at[part], child_sem.at[at])

    def mixed_out(at):
        part = pl.ds(at * TOKENS, TOKENS)
        return pltpu.make_async_copy(mixed.at[part], mixed_hbm.at[part], mixed_sem.at[at])

    def step(at, _):
        here = pl.ds(pl.multiple_of(at * TOKENS, TOKENS), TOKENS)
        rows = att[here, :].astype(jnp.float32)
        mean = jnp.mean(rows * rows, axis=-1, keepdims=True)
        mixed[here, :] = (rows * lax.rsqrt(mean + EPS) * gain[...]).astype(jnp.bfloat16)
        mixed_out(at).start()
        return 0

    for at in range(STEPS):
        child_out(at).start()
    lax.fori_loop(0, STEPS, step, 0)
    for at in range(STEPS):
        child_out(at).wait()
        mixed_out(at).wait()


def body(queries, key_rows, value_rows, slopes, norm_gain, parents, lengths, parent_states):
    anywhere = pl.BlockSpec(memory_space=pl.ANY)
    vmem = pl.BlockSpec(memory_space=pltpu.VMEM)
    dma = pltpu.SemaphoreType.DMA
    bf16, f32 = jnp.bfloat16, jnp.float32
    width = HEADS * DIM
    moved = (GROUP, 2, DIM, DIM)
    in_hbm = [
        pltpu.with_memory_space_constraint(a, pltpu.HBM)
        for a in (queries, key_rows, value_rows, slopes, parents, lengths, parent_states)
    ]
    att, child = pl.pallas_call(
        exchange,
        out_shape=(
            jax.ShapeDtypeStruct((SEG, width), bf16),
            jax.ShapeDtypeStruct(moved, f32),
        ),
        in_specs=[anywhere] * 7,
        out_specs=(vmem,) * 2,
        scratch_shapes=[
            pltpu.VMEM((SEG, width), bf16),
            pltpu.VMEM((SEG, width), bf16),
            pltpu.VMEM((SEG, width), bf16),
            pltpu.SMEM((HEADS,), f32),
            pltpu.SMEM((GROUP,), jnp.int32),
            pltpu.SMEM((GROUP,), jnp.int32),
            pltpu.VMEM((2, 2, DIM, DIM), f32),
            pltpu.VMEM((SEG, width), f32),
            pltpu.VMEM((SEG, SEG), f32),
            pltpu.VMEM(moved, bf16),
            pltpu.VMEM(moved, bf16),
            pltpu.VMEM((2, 2 * SIDE * SIDE, DIM, DIM), bf16),
            pltpu.VMEM((2, 2 * SIDE * SIDE, DIM, DIM), bf16),
            pltpu.VMEM(moved, bf16),
            pltpu.VMEM(moved, bf16),
            pltpu.VMEM(moved, bf16),
            dma((3, CUTS)),
            dma((4,)),
            dma((2,)),
            dma((4, SIDE - 1)),
            dma((4, SIDE, SIDE - 1)),
            dma((4, SIDE * SIDE)),
            dma((GROUP,)),
            dma((GROUP,)),
            dma((GROUP,)),
            dma((GROUP,)),
            dma((GROUP,)),
        ],
        compiler_params=pltpu.CompilerParams(
            collective_id=0, has_side_effects=True, vmem_limit_bytes=40 * 1024 * 1024
        ),
        name="exchange",
    )(*in_hbm)
    mixed, child = pl.pallas_call(
        settle,
        out_shape=(
            jax.ShapeDtypeStruct((SEG, width), bf16),
            jax.ShapeDtypeStruct(moved, f32),
        ),
        in_specs=[vmem] * 3,
        out_specs=(anywhere,) * 2,
        scratch_shapes=[
            pltpu.VMEM((SEG, width), bf16),
            dma((STEPS,)),
            dma((STEPS,)),
        ],
        compiler_params=pltpu.CompilerParams(vmem_limit_bytes=32 * 1024 * 1024),
        name="settle",
    )(att, child, norm_gain.reshape(1, width))
    return mixed, child


def solution(mesh):
    in_specs = (
        P(("dp", "expert"), None),
        P(("dp", "expert"), None),
        P(("dp", "expert"), None),
        P(),
        P(),
        P("dp"),
        P("dp"),
        P("dp", "expert", None, None),
    )
    out_specs = (P(("dp", "expert"), None), P("dp", "expert", None, None))
    return jax.shard_map(body, mesh=mesh, in_specs=in_specs, out_specs=out_specs, check_vma=False)
```

```python
import jax
import jax.numpy as jnp
from jax import lax
from jax.experimental import pallas as pl
from jax.experimental.pallas import tpu as pltpu
from jax.sharding import PartitionSpec as P

EPS = 1e-06
MESH = pl.DeviceIdType.MESH
SIDE = 4
RING = 8
GROUP = 16
HEADS = 32
DIM = 128
SEG = 256
PAIR = 2 * DIM
CUTS = 4
FAR = 1e9
SWAP = 3
EARLY, MIDDLE = 10, 22


def ring_step(i):
    j = i // 2
    off = RING // 2 + ((j + 1) // 2) * (1 - 2 * (j % 2))
    return off, (i + 1) % 2


def exchange(
    q_hbm, k_hbm, v_hbm, slopes_hbm, parents_hbm, lengths_hbm, states_hbm,
    att, child,
    q, k, v, slopes, parents, lengths, states, total, offsets, sent_u, got_u, bank_own, bank_far, picked, passed, got_s,
    load_sem, small_sem, swap_sem, bank_send, bank_hop, bank_recv, u_send, u_recv, s_send, p_send, s_recv,
):
    me_d = lax.axis_index("dp")
    me_e = lax.axis_index("expert")
    y, x = me_d // SIDE, me_d % SIDE
    z, core = me_e // 2, me_e % 2

    arrays = ((k_hbm, k), (v_hbm, v), (q_hbm, q))

    def load(n, cut):
        rows = pl.ds(cut * (SEG // CUTS), SEG // CUTS)
        src, dst = arrays[n]
        return pltpu.make_async_copy(src.at[rows], dst.at[rows], load_sem.at[n, cut])

    def along(slot, j):
        return y * SIDE + (x + j) % SIDE if slot % 2 == 0 else ((y + j) % SIDE) * SIDE + x

    barrier = pltpu.get_barrier_semaphore()

    def greet(i, _):
        pl.semaphore_signal(
            barrier, inc=1, device_id=(me_d, (me_e + i) % GROUP), device_id_type=MESH
        )
        return 0

    lax.fori_loop(1, GROUP, greet, 0)
    for slot in range(2):
        for j in range(1, SIDE):
            pl.semaphore_signal(
                barrier, inc=1, device_id=(along(slot, j), me_e), device_id_type=MESH
            )

    smalls = [
        pltpu.make_async_copy(src, dst, small_sem.at[n])
        for n, (src, dst) in enumerate(
            ((states_hbm, states), (slopes_hbm, slopes), (lengths_hbm, lengths), (parents_hbm, parents))
        )
    ]
    for small in smalls:
        small.start()
    for n in range(3):
        for cut in range(CUTS):
            load(n, cut).start()

    smalls[0].wait()

    for slot in range(2):
        for parent in range(2):
            bank_own[slot, 2 * me_d + parent] = states[parent, slot].astype(jnp.bfloat16)

    def head_columns(e, head):
        return pl.ds(pl.multiple_of(e * PAIR + head * DIM, DIM), DIM)

    def device(off, flip):
        return 2 * ((z + off) % RING) + (core + flip) % 2

    def partner(i):
        return device(*ring_step(i))

    def source(i):
        off, flip = ring_step(i)
        return device(RING - off, flip)

    def giver(slot, i):
        n = i // 2
        up = 1 + 7 * n - 2 * n * n
        return device(up + slot * (RING - 2 * up), i % 2)

    def taker(slot, i):
        return giver(1 - slot, i)

    def kept_for(e, slot):
        return (e + 2 * SWAP + slot * (GROUP - 4 * SWAP)) % GROUP

    other = device(0, 1)

    pl.semaphore_wait(barrier, GROUP - 1 + 2 * (SIDE - 1))

    def swap(slot):
        return pltpu.make_async_remote_copy(
            src_ref=bank_own.at[slot, pl.ds(2 * me_d, 2)],
            dst_ref=bank_far.at[slot, pl.ds(2 * me_d, 2)],
            send_sem=swap_sem.at[0, slot], recv_sem=swap_sem.at[1, slot],
            device_id=(me_d, device(SWAP if slot else RING - SWAP, 0)), device_id_type=MESH,
        )

    swap(0).start()
    swap(1).start()

    def bank_copy(slot, d, to, sem):
        block = (bank_own, bank_far)[slot // 2].at[slot % 2, pl.ds(2 * d, 2)]
        return pltpu.make_async_remote_copy(
            src_ref=block, dst_ref=block, send_sem=sem,
            recv_sem=bank_recv.at[slot, d], device_id=(to, me_e), device_id_type=MESH,
        )

    def first_hop(slot, j):
        return bank_copy(slot, me_d, along(slot, j), bank_send.at[slot, j - 1])

    def second_hop(slot, b, j):
        return bank_copy(slot, along(slot, b), along(slot + 1, j), bank_hop.at[slot, b, j - 1])

    def arrival(slot, d):
        bank_copy(slot, d, along(0, 1), bank_send.at[slot, 0]).wait_recv()

    def open_gather(slots):
        for slot in slots:
            for j in range(1, SIDE):
                first_hop(slot, j).start()
        for slot in slots:
            for j in range(1, SIDE):
                second_hop(slot, 0, j).start()

    def pass_on(slots):
        for b in range(1, SIDE):
            for slot in slots:
                arrival(slot, along(slot, b))
                for j in range(1, SIDE):
                    second_hop(slot, b, j).start()

    def close_gather(slots):
        for j in range(1, SIDE):
            for b in range(SIDE):
                for slot in slots:
                    if slot % 2 == 0:
                        arrival(slot, ((y + j) % SIDE) * SIDE + (x + b) % SIDE)
                    else:
                        arrival(slot, ((y + b) % SIDE) * SIDE + (x + j) % SIDE)

    open_gather((0, 1))

    for small in smalls[1:]:
        small.wait()

    length = lengths[me_e]
    place = lax.broadcasted_iota(jnp.int32, (SEG, DIM), 0)
    remain = (length - 1 - place).astype(jnp.float32)
    inside = place < length
    step_of = (place + 1).astype(jnp.float32)

    def update(e):
        for head in range(2):
            cols = head_columns(e, head)
            slope = slopes[2 * e + head]
            fade = jnp.where(remain >= 0.0, jnp.exp(-slope * jnp.maximum(remain, 0.0)), 0.0)
            keys = (k[:, cols].astype(jnp.float32) * fade).astype(jnp.bfloat16)
            sent_u[e, head] = lax.dot_general(
                keys, v[:, cols], (((0,), (0,)), ((), ())), preferred_element_type=jnp.float32
            ).astype(jnp.bfloat16)

    for cut in range(CUTS):
        load(0, cut).wait()
        load(1, cut).wait()
    update(partner(0))

    def send_u(e):
        return pltpu.make_async_remote_copy(
            src_ref=sent_u.at[e], dst_ref=got_u.at[me_e], send_sem=u_send.at[e],
            recv_sem=u_recv.at[me_e], device_id=(me_d, e), device_id_type=MESH,
        )

    def recv_u(e):
        return pltpu.make_async_remote_copy(
            src_ref=sent_u.at[e], dst_ref=got_u.at[e], send_sem=u_send.at[e],
            recv_sem=u_recv.at[e], device_id=(me_d, e), device_id_type=MESH,
        )

    def send_own(e, slot):
        return pltpu.make_async_remote_copy(
            src_ref=picked.at[e, slot], dst_ref=got_s.at[me_e, slot], send_sem=s_send.at[e, slot],
            recv_sem=s_recv.at[me_e, slot], device_id=(me_d, e), device_id_type=MESH,
        )

    def send_far(e, slot):
        owner = kept_for(me_e, slot)
        return pltpu.make_async_remote_copy(
            src_ref=passed.at[e, slot], dst_ref=got_s.at[owner, slot], send_sem=p_send.at[e, slot],
            recv_sem=s_recv.at[owner, slot], device_id=(me_d, e), device_id_type=MESH,
        )

    def recv_s(e, slot):
        return pltpu.make_async_remote_copy(
            src_ref=picked.at[e, slot], dst_ref=got_s.at[e, slot], send_sem=s_send.at[e, slot],
            recv_sem=s_recv.at[e, slot], device_id=(me_d, e), device_id_type=MESH,
        )

    def update_step(i, _):
        send_u(partner(i)).start()
        update(partner(i + 1))
        return 0

    lax.fori_loop(0, GROUP - 1, update_step, 0)

    pass_on((0, 1))
    swap(0).wait_recv()
    swap(1).wait_recv()
    open_gather((2, 3))

    t_of = lax.broadcasted_iota(jnp.int32, (SEG, SEG), 0)
    s_of = lax.broadcasted_iota(jnp.int32, (SEG, SEG), 1)
    offsets[...] = jnp.where(t_of >= s_of, (t_of - s_of).astype(jnp.float32), FAR)

    for cut in range(CUTS):
        load(2, cut).wait()

    def within(i, _):
        cols = pl.ds(pl.multiple_of(i * DIM, DIM), DIM)
        decay = jnp.exp(-slopes[i] * offsets[...])
        scores = lax.dot_general(
            q[:, cols], k[:, cols], (((1,), (1,)), ((), ())), preferred_element_type=jnp.float32
        )
        total[:, cols] = jnp.dot(
            (scores * decay).astype(jnp.bfloat16), v[:, cols], preferred_element_type=jnp.float32
        )
        return 0

    lax.fori_loop(0, EARLY, within, 0)
    pass_on((2, 3))
    lax.fori_loop(EARLY, MIDDLE, within, 0)

    def pick(e, _):
        parent = parents[e]
        for slot in range(2):
            picked[e, slot] = bank_own[slot, parent]
        return 0

    def each_other(step):
        def both(i, _):
            for slot in range(2):
                step(slot, i)
            return 0

        lax.fori_loop(0, 6, both, 0)

    close_gather((0, 1))
    lax.fori_loop(0, GROUP, pick, 0)
    each_other(lambda slot, i: send_own(taker(slot, i), slot).start())
    for slot in range(2):
        send_own(other, slot).start()

    lax.fori_loop(MIDDLE, HEADS, within, 0)

    def grow(e, fresh):
        for head in range(2):
            fade = jnp.exp(
                jnp.full((1, DIM), -slopes[2 * me_e + head] * lengths[e].astype(jnp.float32), jnp.float32)
            )
            child[e, head] = fade * picked[e, head].astype(jnp.float32) + fresh[e, head].astype(
                jnp.float32
            )

    def grow_step(i, _):
        e = source(i)
        recv_u(e).wait_recv()
        send_u(partner(i)).wait_send()
        grow(e, got_u)
        return 0

    def select(e, slot):
        passed[e, slot] = bank_far[slot, parents[e]]

    def pass_far(slot, i):
        e = giver(slot, i)
        select(e, slot)
        send_far(e, slot).start()

    close_gather((2, 3))
    each_other(pass_far)
    for slot in range(2):
        select(other, slot)
        send_far(other, slot).start()
        select(me_e, slot)

    def finish(owner, slot, src, at):
        cols = head_columns(owner, slot)
        lead = jnp.exp(-slopes[2 * owner + slot] * step_of)
        carried = jnp.dot(q[:, cols], src[at, slot], preferred_element_type=jnp.float32)
        att[:, cols] = jnp.where(inside, total[:, cols] + carried * lead, 0.0).astype(jnp.bfloat16)

    def arrived(owner, slot):
        recv_s(owner, slot).wait_recv()
        finish(owner, slot, got_s, owner)

    def finish_here(slot, _):
        finish(me_e, slot, picked, me_e)
        finish(kept_for(me_e, slot), slot, passed, me_e)
        return 0

    def finish_other(slot, _):
        send_own(other, slot).wait_send()
        send_far(other, slot).wait_send()
        arrived(other, slot)
        arrived(kept_for(other, slot), slot)
        return 0

    def finish_own(j, _):
        i, slot = j // 2, j % 2
        arrived(giver(slot, i), slot)
        send_own(taker(slot, i), slot).wait_send()
        return 0

    def finish_far(j, _):
        i, slot = j // 2, j % 2
        arrived(kept_for(taker(slot, i), slot), slot)
        send_far(giver(slot, i), slot).wait_send()
        return 0

    lax.fori_loop(0, 2, finish_here, 0)
    swap(0).wait_send()
    swap(1).wait_send()
    for slot in range(4):
        for j in range(1, SIDE):
            first_hop(slot, j).wait_send()
            for b in range(SIDE):
                second_hop(slot, b, j).wait_send()
    grow(me_e, sent_u)
    lax.fori_loop(0, GROUP - 1, grow_step, 0)
    lax.fori_loop(0, 2, finish_other, 0)
    lax.fori_loop(0, 12, finish_own, 0)
    lax.fori_loop(0, 12, finish_far, 0)


STEPS = 4
TOKENS = SEG // STEPS


def settle(att, child, gain, mixed_hbm, child_hbm, mixed, child_sem, mixed_sem):
    kids = GROUP // STEPS

    def child_out(at):
        part = pl.ds(at * kids, kids)
        return pltpu.make_async_copy(child.at[part], child_hbm.at[part], child_sem.at[at])

    def mixed_out(at):
        part = pl.ds(at * TOKENS, TOKENS)
        return pltpu.make_async_copy(mixed.at[part], mixed_hbm.at[part], mixed_sem.at[at])

    def step(at, _):
        here = pl.ds(pl.multiple_of(at * TOKENS, TOKENS), TOKENS)
        rows = att[here, :].astype(jnp.float32)
        mean = jnp.mean(rows * rows, axis=-1, keepdims=True)
        mixed[here, :] = (rows * lax.rsqrt(mean + EPS) * gain[...]).astype(jnp.bfloat16)
        mixed_out(at).start()
        return 0

    for at in range(STEPS):
        child_out(at).start()
    lax.fori_loop(0, STEPS, step, 0)
    for at in range(STEPS):
        child_out(at).wait()
        mixed_out(at).wait()


def body(queries, key_rows, value_rows, slopes, norm_gain, parents, lengths, parent_states):
    anywhere = pl.BlockSpec(memory_space=pl.ANY)
    vmem = pl.BlockSpec(memory_space=pltpu.VMEM)
    dma = pltpu.SemaphoreType.DMA
    bf16, f32 = jnp.bfloat16, jnp.float32
    width = HEADS * DIM
    moved = (GROUP, 2, DIM, DIM)
    in_hbm = [
        pltpu.with_memory_space_constraint(a, pltpu.HBM)
        for a in (queries, key_rows, value_rows, slopes, parents, lengths, parent_states)
    ]
    att, child = pl.pallas_call(
        exchange,
        out_shape=(
            jax.ShapeDtypeStruct((SEG, width), bf16),
            jax.ShapeDtypeStruct(moved, f32),
        ),
        in_specs=[anywhere] * 7,
        out_specs=(vmem,) * 2,
        scratch_shapes=[
            pltpu.VMEM((SEG, width), bf16),
            pltpu.VMEM((SEG, width), bf16),
            pltpu.VMEM((SEG, width), bf16),
            pltpu.SMEM((HEADS,), f32),
            pltpu.SMEM((GROUP,), jnp.int32),
            pltpu.SMEM((GROUP,), jnp.int32),
            pltpu.VMEM((2, 2, DIM, DIM), f32),
            pltpu.VMEM((SEG, width), f32),
            pltpu.VMEM((SEG, SEG), f32),
            pltpu.VMEM(moved, bf16),
            pltpu.VMEM(moved, bf16),
            pltpu.VMEM((2, 2 * SIDE * SIDE, DIM, DIM), bf16),
            pltpu.VMEM((2, 2 * SIDE * SIDE, DIM, DIM), bf16),
            pltpu.VMEM(moved, bf16),
            pltpu.VMEM(moved, bf16),
            pltpu.VMEM(moved, bf16),
            dma((3, CUTS)),
            dma((4,)),
            dma((2, 2)),
            dma((4, SIDE - 1)),
            dma((4, SIDE, SIDE - 1)),
            dma((4, SIDE * SIDE)),
            dma((GROUP,)),
            dma((GROUP,)),
            dma((GROUP, 2)),
            dma((GROUP, 2)),
            dma((GROUP, 2)),
        ],
        compiler_params=pltpu.CompilerParams(
            collective_id=0, has_side_effects=True, vmem_limit_bytes=40 * 1024 * 1024
        ),
        name="exchange",
    )(*in_hbm)
    mixed, child = pl.pallas_call(
        settle,
        out_shape=(
            jax.ShapeDtypeStruct((SEG, width), bf16),
            jax.ShapeDtypeStruct(moved, f32),
        ),
        in_specs=[vmem] * 3,
        out_specs=(anywhere,) * 2,
        scratch_shapes=[
            pltpu.VMEM((SEG, width), bf16),
            dma((STEPS,)),
            dma((STEPS,)),
        ],
        compiler_params=pltpu.CompilerParams(vmem_limit_bytes=32 * 1024 * 1024),
        name="settle",
    )(att, child, norm_gain.reshape(1, width))
    return mixed, child


def solution(mesh):
    in_specs = (
        P(("dp", "expert"), None),
        P(("dp", "expert"), None),
        P(("dp", "expert"), None),
        P(),
        P(),
        P("dp"),
        P("dp"),
        P("dp", "expert", None, None),
    )
    out_specs = (P(("dp", "expert"), None), P("dp", "expert", None, None))
    return jax.shard_map(body, mesh=mesh, in_specs=in_specs, out_specs=out_specs, check_vma=False)
```

```python
import jax
import jax.numpy as jnp
from jax import lax
from jax.experimental import pallas as pl
from jax.experimental.pallas import tpu as pltpu
from jax.sharding import PartitionSpec as P

EPS = 1e-06
MESH = pl.DeviceIdType.MESH
SIDE = 4
RING = 8
GROUP = 16
HEADS = 32
DIM = 128
SEG = 256
PAIR = 2 * DIM
CUTS = 4
FAR = 1e9
SWAP = 3
LAST = 6
EARLY, MIDDLE = 10, 22


def ring_step(i):
    j = i // 2
    off = RING // 2 + ((j + 1) // 2) * (1 - 2 * (j % 2))
    return off, (i + 1) % 2


def exchange(
    q_hbm, k_hbm, v_hbm, slopes_hbm, parents_hbm, lengths_hbm, states_hbm,
    att, child,
    q, k, v, slopes, parents, lengths, states, total, offsets, sent_u, got_u, bank_own, bank_far, picked, passed, got_s,
    load_sem, small_sem, bank_send, swap_recv, first_recv, second_recv, u_sem, s_send, s_recv,
):
    me_d = lax.axis_index("dp")
    me_e = lax.axis_index("expert")
    y, x = me_d // SIDE, me_d % SIDE
    z, core = me_e // 2, me_e % 2

    arrays = ((k_hbm, k), (v_hbm, v), (q_hbm, q))

    def load(n, cut):
        rows = pl.ds(cut * (SEG // CUTS), SEG // CUTS)
        src, dst = arrays[n]
        return pltpu.make_async_copy(src.at[rows], dst.at[rows], load_sem.at[n])

    def loaded(n):
        pltpu.make_async_copy(*arrays[n], load_sem.at[n]).wait()

    def along(slot, j):
        return y * SIDE + (x + j) % SIDE if slot % 2 == 0 else ((y + j) % SIDE) * SIDE + x

    barrier = pltpu.get_barrier_semaphore()

    def greet(i, _):
        pl.semaphore_signal(
            barrier, inc=1, device_id=(me_d, (me_e + i) % GROUP), device_id_type=MESH
        )
        return 0

    lax.fori_loop(1, GROUP, greet, 0)
    for slot in range(2):
        for j in range(1, SIDE):
            pl.semaphore_signal(
                barrier, inc=1, device_id=(along(slot, j), me_e), device_id_type=MESH
            )

    smalls = [
        pltpu.make_async_copy(src, dst, small_sem.at[n])
        for n, (src, dst) in enumerate(
            ((states_hbm, states), (slopes_hbm, slopes), (lengths_hbm, lengths), (parents_hbm, parents))
        )
    ]
    for small in smalls:
        small.start()
    for n in range(3):
        for cut in range(CUTS):
            load(n, cut).start()

    smalls[0].wait()

    for slot in range(2):
        for parent in range(2):
            bank_own[slot, 2 * me_d + parent] = states[parent, slot].astype(jnp.bfloat16)

    def head_columns(e, head):
        return pl.ds(pl.multiple_of(e * PAIR + head * DIM, DIM), DIM)

    def device(off, flip):
        return 2 * ((z + off) % RING) + (core + flip) % 2

    def partner(i):
        return device(*ring_step(i))

    def source(i):
        off, flip = ring_step(i)
        return device(RING - off, flip)

    def giver(slot, i):
        n = i // 2
        up = 1 + 7 * n - 2 * n * n
        return device(up + slot * (RING - 2 * up), i % 2)

    def taker(slot, i):
        return giver(1 - slot, i)

    def kept_for(e, slot):
        return (e + 2 * SWAP + slot * (GROUP - 4 * SWAP)) % GROUP

    other = device(0, 1)

    pl.semaphore_wait(barrier, GROUP - 1 + 2 * (SIDE - 1))

    def swap(slot):
        return pltpu.make_async_remote_copy(
            src_ref=bank_own.at[slot, pl.ds(2 * me_d, 2)],
            dst_ref=bank_far.at[slot, pl.ds(2 * me_d, 2)],
            send_sem=bank_send.at[0], recv_sem=swap_recv.at[0],
            device_id=(me_d, device(SWAP if slot else RING - SWAP, 0)), device_id_type=MESH,
        )

    def batch(ref, sem):
        return pltpu.make_async_remote_copy(
            src_ref=ref, dst_ref=ref, send_sem=sem, recv_sem=sem,
            device_id=(me_d, other), device_id_type=MESH,
        )

    swap(0).start()
    swap(1).start()

    banks = (bank_own, bank_far)

    def bank_copy(slot, d, to, sem):
        block = banks[slot // 2].at[slot % 2, pl.ds(2 * d, 2)]
        return pltpu.make_async_remote_copy(
            src_ref=block, dst_ref=block, send_sem=bank_send.at[slot // 2],
            recv_sem=sem, device_id=(to, me_e), device_id_type=MESH,
        )

    def first_hop(slot, j):
        return bank_copy(slot, me_d, along(slot, j), first_recv.at[slot])

    def second_hop(slot, b, j):
        return bank_copy(slot, along(slot, b), along(slot + 1, j), second_recv.at[slot // 2])

    def open_gather(slots):
        for slot in slots:
            for j in range(1, SIDE):
                first_hop(slot, j).start()
        for slot in slots:
            for j in range(1, SIDE):
                second_hop(slot, 0, j).start()

    def pass_on(slots):
        for slot in slots:
            blocks = banks[slot // 2].at[slot % 2, pl.ds(0, 2 * (SIDE - 1))]
            batch(blocks, first_recv.at[slot]).wait_recv()
            for b in range(1, SIDE):
                for j in range(1, SIDE):
                    second_hop(slot, b, j).start()

    def close_gather(n):
        blocks = banks[n].at[:, pl.ds(0, 2 * SIDE * (SIDE - 1))]
        batch(blocks, second_recv.at[n]).wait_recv()

    open_gather((0, 1))

    for small in smalls[1:]:
        small.wait()

    length = lengths[me_e]
    place = lax.broadcasted_iota(jnp.int32, (SEG, DIM), 0)
    remain = (length - 1 - place).astype(jnp.float32)
    inside = place < length
    step_of = (place + 1).astype(jnp.float32)

    def update(e):
        for head in range(2):
            cols = head_columns(e, head)
            slope = slopes[2 * e + head]
            fade = jnp.where(remain >= 0.0, jnp.exp(-slope * jnp.maximum(remain, 0.0)), 0.0)
            keys = (k[:, cols].astype(jnp.float32) * fade).astype(jnp.bfloat16)
            sent_u[e, head] = lax.dot_general(
                keys, v[:, cols], (((0,), (0,)), ((), ())), preferred_element_type=jnp.float32
            ).astype(jnp.bfloat16)

    loaded(0)
    loaded(1)
    update(partner(0))

    def send_u(e):
        return pltpu.make_async_remote_copy(
            src_ref=sent_u.at[e], dst_ref=got_u.at[me_e], send_sem=u_sem.at[0],
            recv_sem=u_sem.at[1], device_id=(me_d, e), device_id_type=MESH,
        )

    def send_own(e, slot, i):
        return pltpu.make_async_remote_copy(
            src_ref=picked.at[e, slot], dst_ref=got_s.at[me_e, slot], send_sem=s_send.at[0],
            recv_sem=s_recv.at[0, i], device_id=(me_d, e), device_id_type=MESH,
        )

    def send_far(e, slot, i):
        owner = kept_for(me_e, slot)
        return pltpu.make_async_remote_copy(
            src_ref=passed.at[e, slot], dst_ref=got_s.at[owner, slot], send_sem=s_send.at[1],
            recv_sem=s_recv.at[1, i], device_id=(me_d, e), device_id_type=MESH,
        )

    def update_step(i, _):
        send_u(partner(i)).start()
        update(partner(i + 1))
        return 0

    lax.fori_loop(0, GROUP - 1, update_step, 0)

    pass_on((0, 1))
    batch(bank_far.at[:, pl.ds(0, 2)], swap_recv.at[0]).wait_recv()
    open_gather((2, 3))

    t_of = lax.broadcasted_iota(jnp.int32, (SEG, SEG), 0)
    s_of = lax.broadcasted_iota(jnp.int32, (SEG, SEG), 1)
    offsets[...] = jnp.where(t_of >= s_of, (t_of - s_of).astype(jnp.float32), FAR)

    loaded(2)

    def within(i, _):
        cols = pl.ds(pl.multiple_of(i * DIM, DIM), DIM)
        decay = jnp.exp(-slopes[i] * offsets[...])
        scores = lax.dot_general(
            q[:, cols], k[:, cols], (((1,), (1,)), ((), ())), preferred_element_type=jnp.float32
        )
        total[:, cols] = jnp.dot(
            (scores * decay).astype(jnp.bfloat16), v[:, cols], preferred_element_type=jnp.float32
        )
        return 0

    lax.fori_loop(0, EARLY, within, 0)
    pass_on((2, 3))
    lax.fori_loop(EARLY, MIDDLE, within, 0)

    def pick(e, _):
        parent = parents[e]
        for slot in range(2):
            picked[e, slot] = bank_own[slot, parent]
        return 0

    def each_other(step):
        def both(i, _):
            for slot in range(2):
                step(slot, i)
            return 0

        lax.fori_loop(0, LAST, both, 0)

    close_gather(0)
    lax.fori_loop(0, GROUP, pick, 0)
    each_other(lambda slot, i: send_own(taker(slot, i), slot, i).start())
    for slot in range(2):
        send_own(other, slot, LAST).start()

    lax.fori_loop(MIDDLE, HEADS, within, 0)

    def grow(e, fresh):
        for head in range(2):
            fade = jnp.exp(
                jnp.full((1, DIM), -slopes[2 * me_e + head] * lengths[e].astype(jnp.float32), jnp.float32)
            )
            child[e, head] = fade * picked[e, head].astype(jnp.float32) + fresh[e, head].astype(
                jnp.float32
            )

    def grow_step(i, _):
        e = source(i)
        grow(e, got_u)
        return 0

    def select(e, slot):
        passed[e, slot] = bank_far[slot, parents[e]]

    def pass_far(slot, i):
        e = giver(slot, i)
        select(e, slot)
        send_far(e, slot, i).start()

    close_gather(1)
    each_other(pass_far)
    for slot in range(2):
        select(other, slot)
        send_far(other, slot, LAST).start()
        select(me_e, slot)

    def finish(owner, slot, src, at):
        cols = head_columns(owner, slot)
        lead = jnp.exp(-slopes[2 * owner + slot] * step_of)
        carried = jnp.dot(q[:, cols], src[at, slot], preferred_element_type=jnp.float32)
        att[:, cols] = jnp.where(inside, total[:, cols] + carried * lead, 0.0).astype(jnp.bfloat16)

    def finish_here(slot, _):
        finish(me_e, slot, picked, me_e)
        finish(kept_for(me_e, slot), slot, passed, me_e)
        return 0

    def arrived(kind, i):
        batch(got_s.at[0], s_recv.at[kind, i]).wait_recv()

    def finish_other(slot, _):
        for owner in (other, kept_for(other, slot)):
            finish(owner, slot, got_s, owner)
        return 0

    def finish_own(i, _):
        arrived(0, i)
        for slot in range(2):
            owner = giver(slot, i)
            finish(owner, slot, got_s, owner)
        return 0

    def finish_far(i, _):
        arrived(1, i)
        for slot in range(2):
            owner = kept_for(taker(slot, i), slot)
            finish(owner, slot, got_s, owner)
        return 0

    lax.fori_loop(0, 2, finish_here, 0)
    batch(bank_own, bank_send.at[0]).wait_send()
    batch(bank_far.at[:, pl.ds(0, 2 * SIDE * SIDE - 2)], bank_send.at[1]).wait_send()
    batch(sent_u.at[pl.ds(0, GROUP - 1)], u_sem.at[0]).wait_send()
    batch(got_u.at[pl.ds(0, GROUP - 1)], u_sem.at[1]).wait_recv()
    grow(me_e, sent_u)
    lax.fori_loop(0, GROUP - 1, grow_step, 0)
    for kind in range(2):
        arrived(kind, LAST)
    lax.fori_loop(0, 2, finish_other, 0)
    lax.fori_loop(0, LAST, finish_own, 0)
    batch(picked.at[pl.ds(0, LAST + 1)], s_send.at[0]).wait_send()
    lax.fori_loop(0, LAST, finish_far, 0)
    batch(passed.at[pl.ds(0, LAST + 1)], s_send.at[1]).wait_send()


STEPS = 4
TOKENS = SEG // STEPS


def settle(att, child, gain, mixed_hbm, child_hbm, mixed, sem):
    kids = GROUP // STEPS

    def child_out(at):
        part = pl.ds(at * kids, kids)
        return pltpu.make_async_copy(child.at[part], child_hbm.at[part], sem.at[0])

    def mixed_out(at):
        part = pl.ds(at * TOKENS, TOKENS)
        return pltpu.make_async_copy(mixed.at[part], mixed_hbm.at[part], sem.at[1])

    def step(at, _):
        here = pl.ds(pl.multiple_of(at * TOKENS, TOKENS), TOKENS)
        rows = att[here, :].astype(jnp.float32)
        mean = jnp.mean(rows * rows, axis=-1, keepdims=True)
        mixed[here, :] = (rows * lax.rsqrt(mean + EPS) * gain[...]).astype(jnp.bfloat16)
        mixed_out(at).start()
        return 0

    for at in range(STEPS):
        child_out(at).start()
    lax.fori_loop(0, STEPS, step, 0)
    pltpu.make_async_copy(child, child_hbm, sem.at[0]).wait()
    pltpu.make_async_copy(mixed, mixed_hbm, sem.at[1]).wait()


def body(queries, key_rows, value_rows, slopes, norm_gain, parents, lengths, parent_states):
    anywhere = pl.BlockSpec(memory_space=pl.ANY)
    vmem = pl.BlockSpec(memory_space=pltpu.VMEM)
    dma = pltpu.SemaphoreType.DMA
    bf16, f32 = jnp.bfloat16, jnp.float32
    width = HEADS * DIM
    moved = (GROUP, 2, DIM, DIM)
    in_hbm = [
        pltpu.with_memory_space_constraint(a, pltpu.HBM)
        for a in (queries, key_rows, value_rows, slopes, parents, lengths, parent_states)
    ]
    att, child = pl.pallas_call(
        exchange,
        out_shape=(
            jax.ShapeDtypeStruct((SEG, width), bf16),
            jax.ShapeDtypeStruct(moved, f32),
        ),
        in_specs=[anywhere] * 7,
        out_specs=(vmem,) * 2,
        scratch_shapes=[
            pltpu.VMEM((SEG, width), bf16),
            pltpu.VMEM((SEG, width), bf16),
            pltpu.VMEM((SEG, width), bf16),
            pltpu.SMEM((HEADS,), f32),
            pltpu.SMEM((GROUP,), jnp.int32),
            pltpu.SMEM((GROUP,), jnp.int32),
            pltpu.VMEM((2, 2, DIM, DIM), f32),
            pltpu.VMEM((SEG, width), f32),
            pltpu.VMEM((SEG, SEG), f32),
            pltpu.VMEM(moved, bf16),
            pltpu.VMEM(moved, bf16),
            pltpu.VMEM((2, 2 * SIDE * SIDE, DIM, DIM), bf16),
            pltpu.VMEM((2, 2 * SIDE * SIDE, DIM, DIM), bf16),
            pltpu.VMEM(moved, bf16),
            pltpu.VMEM(moved, bf16),
            pltpu.VMEM(moved, bf16),
            dma((3,)),
            dma((4,)),
            dma((2,)),
            dma((1,)),
            dma((4,)),
            dma((2,)),
            dma((2,)),
            dma((2,)),
            dma((2, LAST + 1)),
        ],
        compiler_params=pltpu.CompilerParams(
            collective_id=0, has_side_effects=True, vmem_limit_bytes=40 * 1024 * 1024
        ),
        name="exchange",
    )(*in_hbm)
    mixed, child = pl.pallas_call(
        settle,
        out_shape=(
            jax.ShapeDtypeStruct((SEG, width), bf16),
            jax.ShapeDtypeStruct(moved, f32),
        ),
        in_specs=[vmem] * 3,
        out_specs=(anywhere,) * 2,
        scratch_shapes=[
            pltpu.VMEM((SEG, width), bf16),
            dma((2,)),
        ],
        compiler_params=pltpu.CompilerParams(vmem_limit_bytes=32 * 1024 * 1024),
        name="settle",
    )(att, child, norm_gain.reshape(1, width))
    return mixed, child


def solution(mesh):
    in_specs = (
        P(("dp", "expert"), None),
        P(("dp", "expert"), None),
        P(("dp", "expert"), None),
        P(),
        P(),
        P("dp"),
        P("dp"),
        P("dp", "expert", None, None),
    )
    out_specs = (P(("dp", "expert"), None), P("dp", "expert", None, None))
    return jax.shard_map(body, mesh=mesh, in_specs=in_specs, out_specs=out_specs, check_vma=False)
```

```python
import jax
import jax.numpy as jnp
from jax import lax
from jax.experimental import pallas as pl
from jax.experimental.pallas import tpu as pltpu
from jax.sharding import PartitionSpec as P

EPS = 1e-06
MESH = pl.DeviceIdType.MESH
SIDE = 4
RING = 8
GROUP = 16
HEADS = 32
DIM = 128
SEG = 256
PAIR = 2 * DIM
CUTS = 4
FAR = 1e9
SWAP = 3
LAST = 6
EARLY, MIDDLE = 10, 22


def ring_step(i):
    j = i // 2
    off = RING // 2 + ((j + 1) // 2) * (1 - 2 * (j % 2))
    return off, (i + 1) % 2


def exchange(
    q_hbm, k_hbm, v_hbm, slopes_hbm, parents_hbm, lengths_hbm, states_hbm,
    att, child,
    q, k, v, slopes, parents, lengths, states, total, offsets, sent_u, got_u, bank_own, bank_far, picked, passed, got_s,
    load_sem, small_sem, bank_send, swap_recv, first_recv, second_recv, u_sem, s_send, s_recv,
):
    me_d = lax.axis_index("dp")
    me_e = lax.axis_index("expert")
    y, x = me_d // SIDE, me_d % SIDE
    z, core = me_e // 2, me_e % 2

    arrays = ((k_hbm, k), (v_hbm, v), (q_hbm, q))

    def load(n, cut):
        rows = pl.ds(cut * (SEG // CUTS), SEG // CUTS)
        src, dst = arrays[n]
        return pltpu.make_async_copy(src.at[rows], dst.at[rows], load_sem.at[n])

    def loaded(n):
        pltpu.make_async_copy(*arrays[n], load_sem.at[n]).wait()

    def along(slot, j):
        return y * SIDE + (x + j) % SIDE if slot % 2 == 0 else ((y + j) % SIDE) * SIDE + x

    barrier = pltpu.get_barrier_semaphore()

    def greet(d, e):
        pl.semaphore_signal(barrier, inc=1, device_id=(d, e), device_id_type=MESH)

    for i in range(6):
        off, flip = ring_step(i)
        greet(me_d, 2 * ((z + off) % RING) + (core + flip) % 2)
    for j in (2, 1, 3):
        for slot in range(2):
            greet(along(slot, j), me_e)
    for i in range(6, GROUP - 1):
        off, flip = ring_step(i)
        greet(me_d, 2 * ((z + off) % RING) + (core + flip) % 2)

    smalls = [
        pltpu.make_async_copy(src, dst, small_sem.at[n])
        for n, (src, dst) in enumerate(
            ((states_hbm, states), (slopes_hbm, slopes), (lengths_hbm, lengths), (parents_hbm, parents))
        )
    ]
    for small in smalls:
        small.start()
    for n in range(3):
        for cut in range(CUTS):
            load(n, cut).start()

    smalls[0].wait()

    for slot in range(2):
        for parent in range(2):
            bank_own[slot, 2 * me_d + parent] = states[parent, slot].astype(jnp.bfloat16)

    def head_columns(e, head):
        return pl.ds(pl.multiple_of(e * PAIR + head * DIM, DIM), DIM)

    def device(off, flip):
        return 2 * ((z + off) % RING) + (core + flip) % 2

    def partner(i):
        return device(*ring_step(i))

    def source(i):
        off, flip = ring_step(i)
        return device(RING - off, flip)

    def giver(slot, i):
        n = i // 2
        up = 1 + 7 * n - 2 * n * n
        return device(up + slot * (RING - 2 * up), i % 2)

    def taker(slot, i):
        return giver(1 - slot, i)

    def kept_for(e, slot):
        return (e + 2 * SWAP + slot * (GROUP - 4 * SWAP)) % GROUP

    other = device(0, 1)

    pl.semaphore_wait(barrier, GROUP - 1 + 2 * (SIDE - 1))

    def swap(slot):
        return pltpu.make_async_remote_copy(
            src_ref=bank_own.at[slot, pl.ds(2 * me_d, 2)],
            dst_ref=bank_far.at[slot, pl.ds(2 * me_d, 2)],
            send_sem=bank_send.at[0], recv_sem=swap_recv.at[0],
            device_id=(me_d, device(SWAP if slot else RING - SWAP, 0)), device_id_type=MESH,
        )

    def batch(ref, sem):
        return pltpu.make_async_remote_copy(
            src_ref=ref, dst_ref=ref, send_sem=sem, recv_sem=sem,
            device_id=(me_d, other), device_id_type=MESH,
        )

    swap(0).start()
    swap(1).start()

    banks = (bank_own, bank_far)

    def bank_copy(slot, d, to, sem):
        block = banks[slot // 2].at[slot % 2, pl.ds(2 * d, 2)]
        return pltpu.make_async_remote_copy(
            src_ref=block, dst_ref=block, send_sem=bank_send.at[slot // 2],
            recv_sem=sem, device_id=(to, me_e), device_id_type=MESH,
        )

    def first_hop(slot, j):
        return bank_copy(slot, me_d, along(slot, j), first_recv.at[slot])

    def second_hop(slot, b, j):
        return bank_copy(slot, along(slot, b), along(slot + 1, j), second_recv.at[slot // 2])

    def open_gather(slots):
        for slot in slots:
            for j in range(1, SIDE):
                first_hop(slot, j).start()
        for slot in slots:
            for j in range(1, SIDE):
                second_hop(slot, 0, j).start()

    def pass_on(slots):
        for slot in slots:
            blocks = banks[slot // 2].at[slot % 2, pl.ds(0, 2 * (SIDE - 1))]
            batch(blocks, first_recv.at[slot]).wait_recv()
            for b in range(1, SIDE):
                for j in range(1, SIDE):
                    second_hop(slot, b, j).start()

    def close_gather(n):
        blocks = banks[n].at[:, pl.ds(0, 2 * SIDE * (SIDE - 1))]
        batch(blocks, second_recv.at[n]).wait_recv()

    open_gather((0, 1))

    for small in smalls[1:]:
        small.wait()

    length = lengths[me_e]
    place = lax.broadcasted_iota(jnp.int32, (SEG, DIM), 0)
    remain = (length - 1 - place).astype(jnp.float32)
    inside = place < length
    step_of = (place + 1).astype(jnp.float32)

    def update(e):
        for head in range(2):
            cols = head_columns(e, head)
            slope = slopes[2 * e + head]
            fade = jnp.where(remain >= 0.0, jnp.exp(-slope * jnp.maximum(remain, 0.0)), 0.0)
            keys = (k[:, cols].astype(jnp.float32) * fade).astype(jnp.bfloat16)
            sent_u[e, head] = lax.dot_general(
                keys, v[:, cols], (((0,), (0,)), ((), ())), preferred_element_type=jnp.float32
            ).astype(jnp.bfloat16)

    loaded(0)
    loaded(1)
    update(partner(0))

    def send_u(e):
        return pltpu.make_async_remote_copy(
            src_ref=sent_u.at[e], dst_ref=got_u.at[me_e], send_sem=u_sem.at[0],
            recv_sem=u_sem.at[1], device_id=(me_d, e), device_id_type=MESH,
        )

    def send_own(e, slot, i):
        return pltpu.make_async_remote_copy(
            src_ref=picked.at[e, slot], dst_ref=got_s.at[me_e, slot], send_sem=s_send.at[0],
            recv_sem=s_recv.at[0, i], device_id=(me_d, e), device_id_type=MESH,
        )

    def send_far(e, slot, i):
        owner = kept_for(me_e, slot)
        return pltpu.make_async_remote_copy(
            src_ref=passed.at[e, slot], dst_ref=got_s.at[owner, slot], send_sem=s_send.at[1],
            recv_sem=s_recv.at[1, i], device_id=(me_d, e), device_id_type=MESH,
        )

    def update_step(i, _):
        send_u(partner(i)).start()
        update(partner(i + 1))
        return 0

    lax.fori_loop(0, GROUP - 1, update_step, 0)

    pass_on((0, 1))
    batch(bank_far.at[:, pl.ds(0, 2)], swap_recv.at[0]).wait_recv()
    open_gather((2, 3))

    t_of = lax.broadcasted_iota(jnp.int32, (SEG, SEG), 0)
    s_of = lax.broadcasted_iota(jnp.int32, (SEG, SEG), 1)
    offsets[...] = jnp.where(t_of >= s_of, (t_of - s_of).astype(jnp.float32), FAR)

    loaded(2)

    def within(i, _):
        cols = pl.ds(pl.multiple_of(i * DIM, DIM), DIM)
        decay = jnp.exp(-slopes[i] * offsets[...])
        scores = lax.dot_general(
            q[:, cols], k[:, cols], (((1,), (1,)), ((), ())), preferred_element_type=jnp.float32
        )
        total[:, cols] = jnp.dot(
            (scores * decay).astype(jnp.bfloat16), v[:, cols], preferred_element_type=jnp.float32
        )
        return 0

    lax.fori_loop(0, EARLY, within, 0)
    pass_on((2, 3))
    lax.fori_loop(EARLY, MIDDLE, within, 0)

    def pick(e, _):
        parent = parents[e]
        for slot in range(2):
            picked[e, slot] = bank_own[slot, parent]
        return 0

    def each_other(step):
        def both(i, _):
            for slot in range(2):
                step(slot, i)
            return 0

        lax.fori_loop(0, LAST, both, 0)

    close_gather(0)
    lax.fori_loop(0, GROUP, pick, 0)
    each_other(lambda slot, i: send_own(taker(slot, i), slot, i).start())
    for slot in range(2):
        send_own(other, slot, LAST).start()

    lax.fori_loop(MIDDLE, HEADS, within, 0)

    def grow(e, fresh):
        for head in range(2):
            fade = jnp.exp(
                jnp.full((1, DIM), -slopes[2 * me_e + head] * lengths[e].astype(jnp.float32), jnp.float32)
            )
            child[e, head] = fade * picked[e, head].astype(jnp.float32) + fresh[e, head].astype(
                jnp.float32
            )

    def grow_step(i, _):
        e = source(i)
        grow(e, got_u)
        return 0

    def select(e, slot):
        passed[e, slot] = bank_far[slot, parents[e]]

    def pass_far(slot, i):
        e = giver(slot, i)
        select(e, slot)
        send_far(e, slot, i).start()

    close_gather(1)
    each_other(pass_far)
    for slot in range(2):
        select(other, slot)
        send_far(other, slot, LAST).start()
        select(me_e, slot)

    def finish(owner, slot, src, at):
        cols = head_columns(owner, slot)
        lead = jnp.exp(-slopes[2 * owner + slot] * step_of)
        carried = jnp.dot(q[:, cols], src[at, slot], preferred_element_type=jnp.float32)
        att[:, cols] = jnp.where(inside, total[:, cols] + carried * lead, 0.0).astype(jnp.bfloat16)

    def finish_here(slot, _):
        finish(me_e, slot, picked, me_e)
        finish(kept_for(me_e, slot), slot, passed, me_e)
        return 0

    def arrived(kind, i):
        batch(got_s.at[0], s_recv.at[kind, i]).wait_recv()

    def finish_other(slot, _):
        for owner in (other, kept_for(other, slot)):
            finish(owner, slot, got_s, owner)
        return 0

    def finish_own(i, _):
        arrived(0, i)
        for slot in range(2):
            owner = giver(slot, i)
            finish(owner, slot, got_s, owner)
        return 0

    def finish_far(i, _):
        arrived(1, i)
        for slot in range(2):
            owner = kept_for(taker(slot, i), slot)
            finish(owner, slot, got_s, owner)
        return 0

    lax.fori_loop(0, 2, finish_here, 0)
    batch(bank_own, bank_send.at[0]).wait_send()
    batch(bank_far.at[:, pl.ds(0, 2 * SIDE * SIDE - 2)], bank_send.at[1]).wait_send()
    batch(sent_u.at[pl.ds(0, GROUP - 1)], u_sem.at[0]).wait_send()
    batch(got_u.at[pl.ds(0, GROUP - 1)], u_sem.at[1]).wait_recv()
    grow(me_e, sent_u)
    lax.fori_loop(0, GROUP - 1, grow_step, 0)
    for kind in range(2):
        arrived(kind, LAST)
    lax.fori_loop(0, 2, finish_other, 0)
    lax.fori_loop(0, LAST, finish_own, 0)
    batch(picked.at[pl.ds(0, LAST + 1)], s_send.at[0]).wait_send()
    lax.fori_loop(0, LAST, finish_far, 0)
    batch(passed.at[pl.ds(0, LAST + 1)], s_send.at[1]).wait_send()


STEPS = 4
TOKENS = SEG // STEPS


def settle(att, child, gain, mixed_hbm, child_hbm, mixed, sem):
    def mixed_out(at):
        part = pl.ds(at * TOKENS, TOKENS)
        return pltpu.make_async_copy(mixed.at[part], mixed_hbm.at[part], sem.at[1])

    def step(at, _):
        here = pl.ds(pl.multiple_of(at * TOKENS, TOKENS), TOKENS)
        rows = att[here, :].astype(jnp.float32)
        mean = jnp.mean(rows * rows, axis=-1, keepdims=True)
        mixed[here, :] = (rows * lax.rsqrt(mean + EPS) * gain[...]).astype(jnp.bfloat16)
        mixed_out(at).start()
        return 0

    child_out = pltpu.make_async_copy(child, child_hbm, sem.at[0])
    child_out.start()
    lax.fori_loop(0, STEPS, step, 0)
    child_out.wait()
    pltpu.make_async_copy(mixed, mixed_hbm, sem.at[1]).wait()


def body(queries, key_rows, value_rows, slopes, norm_gain, parents, lengths, parent_states):
    anywhere = pl.BlockSpec(memory_space=pl.ANY)
    vmem = pl.BlockSpec(memory_space=pltpu.VMEM)
    dma = pltpu.SemaphoreType.DMA
    bf16, f32 = jnp.bfloat16, jnp.float32
    width = HEADS * DIM
    moved = (GROUP, 2, DIM, DIM)
    in_hbm = [
        pltpu.with_memory_space_constraint(a, pltpu.HBM)
        for a in (queries, key_rows, value_rows, slopes, parents, lengths, parent_states)
    ]
    att, child = pl.pallas_call(
        exchange,
        out_shape=(
            jax.ShapeDtypeStruct((SEG, width), bf16),
            jax.ShapeDtypeStruct(moved, f32),
        ),
        in_specs=[anywhere] * 7,
        out_specs=(vmem,) * 2,
        scratch_shapes=[
            pltpu.VMEM((SEG, width), bf16),
            pltpu.VMEM((SEG, width), bf16),
            pltpu.VMEM((SEG, width), bf16),
            pltpu.SMEM((HEADS,), f32),
            pltpu.SMEM((GROUP,), jnp.int32),
            pltpu.SMEM((GROUP,), jnp.int32),
            pltpu.VMEM((2, 2, DIM, DIM), f32),
            pltpu.VMEM((SEG, width), f32),
            pltpu.VMEM((SEG, SEG), f32),
            pltpu.VMEM(moved, bf16),
            pltpu.VMEM(moved, bf16),
            pltpu.VMEM((2, 2 * SIDE * SIDE, DIM, DIM), bf16),
            pltpu.VMEM((2, 2 * SIDE * SIDE, DIM, DIM), bf16),
            pltpu.VMEM(moved, bf16),
            pltpu.VMEM(moved, bf16),
            pltpu.VMEM(moved, bf16),
            dma((3,)),
            dma((4,)),
            dma((2,)),
            dma((1,)),
            dma((4,)),
            dma((2,)),
            dma((2,)),
            dma((2,)),
            dma((2, LAST + 1)),
        ],
        compiler_params=pltpu.CompilerParams(
            collective_id=0, has_side_effects=True, vmem_limit_bytes=40 * 1024 * 1024
        ),
        name="exchange",
    )(*in_hbm)
    mixed, child = pl.pallas_call(
        settle,
        out_shape=(
            jax.ShapeDtypeStruct((SEG, width), bf16),
            jax.ShapeDtypeStruct(moved, f32),
        ),
        in_specs=[vmem] * 3,
        out_specs=(anywhere,) * 2,
        scratch_shapes=[
            pltpu.VMEM((SEG, width), bf16),
            dma((2,)),
        ],
        compiler_params=pltpu.CompilerParams(vmem_limit_bytes=32 * 1024 * 1024),
        name="settle",
    )(att, child, norm_gain.reshape(1, width))
    return mixed, child


def solution(mesh):
    in_specs = (
        P(("dp", "expert"), None),
        P(("dp", "expert"), None),
        P(("dp", "expert"), None),
        P(),
        P(),
        P("dp"),
        P("dp"),
        P("dp", "expert", None, None),
    )
    out_specs = (P(("dp", "expert"), None), P("dp", "expert", None, None))
    return jax.shard_map(body, mesh=mesh, in_specs=in_specs, out_specs=out_specs, check_vma=False)
```

```python
import jax
import jax.numpy as jnp
from jax import lax
from jax.experimental import pallas as pl
from jax.experimental.pallas import tpu as pltpu
from jax.sharding import PartitionSpec as P

EPS = 1e-06
MESH = pl.DeviceIdType.MESH
SIDE = 4
RING = 8
GROUP = 16
HEADS = 32
DIM = 128
SEG = 256
PAIR = 2 * DIM
CUTS = 4
FAR = 1e9
SWAP = 3
LAST = 6
EARLY, MIDDLE = 10, 22


def ring_step(i):
    j = i // 2
    off = RING // 2 + ((j + 1) // 2) * (1 - 2 * (j % 2))
    return off, (i + 1) % 2


def exchange(
    q_hbm, k_hbm, v_hbm, slopes_hbm, parents_hbm, lengths_hbm, states_hbm,
    att, child,
    q, k, v, slopes, parents, lengths, states, total, offsets, sent_u, got_u, bank_own, bank_far, picked, passed, got_s,
    load_sem, small_sem, bank_send, swap_recv, first_recv, second_recv, u_sem, s_send, s_recv,
):
    me_d = lax.axis_index("dp")
    me_e = lax.axis_index("expert")
    y, x = me_d // SIDE, me_d % SIDE
    z, core = me_e // 2, me_e % 2

    arrays = ((k_hbm, k), (v_hbm, v), (q_hbm, q))

    def load(n, cut):
        rows = pl.ds(cut * (SEG // CUTS), SEG // CUTS)
        src, dst = arrays[n]
        return pltpu.make_async_copy(src.at[rows], dst.at[rows], load_sem.at[n])

    def loaded(n):
        pltpu.make_async_copy(*arrays[n], load_sem.at[n]).wait()

    def along(slot, j):
        return y * SIDE + (x + j) % SIDE if slot % 2 == 0 else ((y + j) % SIDE) * SIDE + x

    def spot(slot, b):
        return SIDE * (x if slot % 2 else y) + b

    barrier = pltpu.get_barrier_semaphore()

    def greet(d, e):
        pl.semaphore_signal(barrier, inc=1, device_id=(d, e), device_id_type=MESH)

    for i in range(6):
        off, flip = ring_step(i)
        greet(me_d, 2 * ((z + off) % RING) + (core + flip) % 2)
    for j in (2, 1, 3):
        for slot in range(2):
            greet(along(slot, j), me_e)
    for i in range(6, GROUP - 1):
        off, flip = ring_step(i)
        greet(me_d, 2 * ((z + off) % RING) + (core + flip) % 2)

    smalls = [
        pltpu.make_async_copy(src, dst, small_sem.at[n])
        for n, (src, dst) in enumerate(
            ((states_hbm, states), (slopes_hbm, slopes), (lengths_hbm, lengths), (parents_hbm, parents))
        )
    ]
    for small in smalls:
        small.start()
    for n in range(3):
        for cut in range(CUTS):
            load(n, cut).start()

    smalls[0].wait()

    for slot in range(2):
        for parent in range(2):
            bank_own[slot, 2 * spot(slot, 0) + parent] = states[parent, slot].astype(jnp.bfloat16)

    def head_columns(e, head):
        return pl.ds(pl.multiple_of(e * PAIR + head * DIM, DIM), DIM)

    def device(off, flip):
        return 2 * ((z + off) % RING) + (core + flip) % 2

    def partner(i):
        return device(*ring_step(i))

    def source(i):
        off, flip = ring_step(i)
        return device(RING - off, flip)

    def giver(slot, i):
        n = i // 2
        up = 1 + 7 * n - 2 * n * n
        return device(up + slot * (RING - 2 * up), i % 2)

    def taker(slot, i):
        return giver(1 - slot, i)

    def kept_for(e, slot):
        return (e + 2 * SWAP + slot * (GROUP - 4 * SWAP)) % GROUP

    other = device(0, 1)

    pl.semaphore_wait(barrier, GROUP - 1 + 2 * (SIDE - 1))

    def swap(slot):
        return pltpu.make_async_remote_copy(
            src_ref=bank_own.at[slot, pl.ds(2 * spot(slot, 0), 2)],
            dst_ref=bank_far.at[slot, pl.ds(2 * spot(slot, 0), 2)],
            send_sem=bank_send.at[0], recv_sem=swap_recv.at[0],
            device_id=(me_d, device(SWAP if slot else RING - SWAP, 0)), device_id_type=MESH,
        )

    def batch(ref, sem):
        return pltpu.make_async_remote_copy(
            src_ref=ref, dst_ref=ref, send_sem=sem, recv_sem=sem,
            device_id=(me_d, other), device_id_type=MESH,
        )

    swap(0).start()
    swap(1).start()

    banks = (bank_own, bank_far)

    def bank_copy(slot, src, dst, count, to, sem):
        bank = banks[slot // 2].at[slot % 2]
        return pltpu.make_async_remote_copy(
            src_ref=bank.at[pl.ds(2 * src, 2 * count)], dst_ref=bank.at[pl.ds(2 * dst, 2 * count)],
            send_sem=bank_send.at[slot // 2], recv_sem=sem, device_id=(to, me_e), device_id_type=MESH,
        )

    def first_hop(slot, j):
        to = along(slot, j)
        return bank_copy(slot, spot(slot, 0), spot(slot, SIDE - j), 1, to, first_recv.at[slot])

    def second_hop(slot, b, count, j):
        at, to = spot(slot, b), along(slot + 1, j)
        return bank_copy(slot, at, at, count, to, second_recv.at[slot // 2])

    def open_gather(slots):
        for slot in slots:
            for j in range(1, SIDE):
                first_hop(slot, j).start()
        for slot in slots:
            for j in range(1, SIDE):
                second_hop(slot, 0, 1, j).start()

    def pass_on(slots):
        for slot in slots:
            blocks = banks[slot // 2].at[slot % 2, pl.ds(0, 2 * (SIDE - 1))]
            batch(blocks, first_recv.at[slot]).wait_recv()
            for j in range(1, SIDE):
                second_hop(slot, 1, SIDE - 1, j).start()

    def close_gather(n):
        blocks = banks[n].at[:, pl.ds(0, 2 * SIDE * (SIDE - 1))]
        batch(blocks, second_recv.at[n]).wait_recv()

    open_gather((0, 1))

    for small in smalls[1:]:
        small.wait()

    length = lengths[me_e]
    place = lax.broadcasted_iota(jnp.int32, (SEG, DIM), 0)
    remain = (length - 1 - place).astype(jnp.float32)
    inside = place < length
    step_of = (place + 1).astype(jnp.float32)

    def update(e):
        for head in range(2):
            cols = head_columns(e, head)
            slope = slopes[2 * e + head]
            fade = jnp.where(remain >= 0.0, jnp.exp(-slope * jnp.maximum(remain, 0.0)), 0.0)
            keys = (k[:, cols].astype(jnp.float32) * fade).astype(jnp.bfloat16)
            sent_u[e, head] = lax.dot_general(
                keys, v[:, cols], (((0,), (0,)), ((), ())), preferred_element_type=jnp.float32
            ).astype(jnp.bfloat16)

    loaded(0)
    loaded(1)
    update(partner(0))

    def send_u(e):
        return pltpu.make_async_remote_copy(
            src_ref=sent_u.at[e], dst_ref=got_u.at[me_e], send_sem=u_sem.at[0],
            recv_sem=u_sem.at[1], device_id=(me_d, e), device_id_type=MESH,
        )

    def send_own(e, slot, i):
        return pltpu.make_async_remote_copy(
            src_ref=picked.at[e, slot], dst_ref=got_s.at[me_e, slot], send_sem=s_send.at[0],
            recv_sem=s_recv.at[0, i], device_id=(me_d, e), device_id_type=MESH,
        )

    def send_far(e, slot, i):
        owner = kept_for(me_e, slot)
        return pltpu.make_async_remote_copy(
            src_ref=passed.at[e, slot], dst_ref=got_s.at[owner, slot], send_sem=s_send.at[1],
            recv_sem=s_recv.at[1, i], device_id=(me_d, e), device_id_type=MESH,
        )

    def update_step(i, _):
        send_u(partner(i)).start()
        update(partner(i + 1))
        return 0

    lax.fori_loop(0, GROUP - 1, update_step, 0)

    pass_on((0, 1))
    batch(bank_far.at[:, pl.ds(0, 2)], swap_recv.at[0]).wait_recv()
    open_gather((2, 3))

    t_of = lax.broadcasted_iota(jnp.int32, (SEG, SEG), 0)
    s_of = lax.broadcasted_iota(jnp.int32, (SEG, SEG), 1)
    offsets[...] = jnp.where(t_of >= s_of, (t_of - s_of).astype(jnp.float32), FAR)

    loaded(2)

    def within(i, _):
        cols = pl.ds(pl.multiple_of(i * DIM, DIM), DIM)
        decay = jnp.exp(-slopes[i] * offsets[...])
        scores = lax.dot_general(
            q[:, cols], k[:, cols], (((1,), (1,)), ((), ())), preferred_element_type=jnp.float32
        )
        total[:, cols] = jnp.dot(
            (scores * decay).astype(jnp.bfloat16), v[:, cols], preferred_element_type=jnp.float32
        )
        return 0

    lax.fori_loop(0, EARLY, within, 0)
    pass_on((2, 3))
    lax.fori_loop(EARLY, MIDDLE, within, 0)

    def held(e, slot):
        parent = parents[e]
        half, mine = parent % 2, parent // 2
        down, right = mine // SIDE, mine % SIDE
        row, step = (right, down - y) if slot else (down, right - x)
        return 2 * (SIDE * row + (step + SIDE) % SIDE) + half

    def pick(e, _):
        for slot in range(2):
            picked[e, slot] = bank_own[slot, held(e, slot)]
        return 0

    def each_other(step):
        def both(i, _):
            for slot in range(2):
                step(slot, i)
            return 0

        lax.fori_loop(0, LAST, both, 0)

    close_gather(0)
    lax.fori_loop(0, GROUP, pick, 0)
    each_other(lambda slot, i: send_own(taker(slot, i), slot, i).start())
    for slot in range(2):
        send_own(other, slot, LAST).start()

    lax.fori_loop(MIDDLE, HEADS, within, 0)

    def grow(e, fresh):
        for head in range(2):
            fade = jnp.exp(
                jnp.full((1, DIM), -slopes[2 * me_e + head] * lengths[e].astype(jnp.float32), jnp.float32)
            )
            child[e, head] = fade * picked[e, head].astype(jnp.float32) + fresh[e, head].astype(
                jnp.float32
            )

    def grow_step(i, _):
        e = source(i)
        grow(e, got_u)
        return 0

    def select(e, slot):
        passed[e, slot] = bank_far[slot, held(e, slot)]

    def pass_far(slot, i):
        e = giver(slot, i)
        select(e, slot)
        send_far(e, slot, i).start()

    close_gather(1)
    each_other(pass_far)
    for slot in range(2):
        select(other, slot)
        send_far(other, slot, LAST).start()
        select(me_e, slot)

    def finish(owner, slot, src, at):
        cols = head_columns(owner, slot)
        lead = jnp.exp(-slopes[2 * owner + slot] * step_of)
        carried = jnp.dot(q[:, cols], src[at, slot], preferred_element_type=jnp.float32)
        att[:, cols] = jnp.where(inside, total[:, cols] + carried * lead, 0.0).astype(jnp.bfloat16)

    def finish_here(slot, _):
        finish(me_e, slot, picked, me_e)
        finish(kept_for(me_e, slot), slot, passed, me_e)
        return 0

    def arrived(kind, i):
        batch(got_s.at[0], s_recv.at[kind, i]).wait_recv()

    def finish_other(slot, _):
        for owner in (other, kept_for(other, slot)):
            finish(owner, slot, got_s, owner)
        return 0

    def finish_own(i, _):
        arrived(0, i)
        for slot in range(2):
            owner = giver(slot, i)
            finish(owner, slot, got_s, owner)
        return 0

    def finish_far(i, _):
        arrived(1, i)
        for slot in range(2):
            owner = kept_for(taker(slot, i), slot)
            finish(owner, slot, got_s, owner)
        return 0

    lax.fori_loop(0, 2, finish_here, 0)
    batch(bank_own, bank_send.at[0]).wait_send()
    batch(bank_far.at[:, pl.ds(0, 2 * SIDE * SIDE - 2)], bank_send.at[1]).wait_send()
    batch(sent_u.at[pl.ds(0, GROUP - 1)], u_sem.at[0]).wait_send()
    batch(got_u.at[pl.ds(0, GROUP - 1)], u_sem.at[1]).wait_recv()
    grow(me_e, sent_u)
    lax.fori_loop(0, GROUP - 1, grow_step, 0)
    for kind in range(2):
        arrived(kind, LAST)
    lax.fori_loop(0, 2, finish_other, 0)
    lax.fori_loop(0, LAST, finish_own, 0)
    batch(picked.at[pl.ds(0, LAST + 1)], s_send.at[0]).wait_send()
    lax.fori_loop(0, LAST, finish_far, 0)
    batch(passed.at[pl.ds(0, LAST + 1)], s_send.at[1]).wait_send()


STEPS = 4
TOKENS = SEG // STEPS


def settle(att, child, gain, mixed_hbm, child_hbm, mixed, sem):
    def mixed_out(at):
        part = pl.ds(at * TOKENS, TOKENS)
        return pltpu.make_async_copy(mixed.at[part], mixed_hbm.at[part], sem.at[1])

    def step(at, _):
        here = pl.ds(pl.multiple_of(at * TOKENS, TOKENS), TOKENS)
        rows = att[here, :].astype(jnp.float32)
        mean = jnp.mean(rows * rows, axis=-1, keepdims=True)
        mixed[here, :] = (rows * lax.rsqrt(mean + EPS) * gain[...]).astype(jnp.bfloat16)
        mixed_out(at).start()
        return 0

    child_out = pltpu.make_async_copy(child, child_hbm, sem.at[0])
    child_out.start()
    lax.fori_loop(0, STEPS, step, 0)
    child_out.wait()
    pltpu.make_async_copy(mixed, mixed_hbm, sem.at[1]).wait()


def body(queries, key_rows, value_rows, slopes, norm_gain, parents, lengths, parent_states):
    anywhere = pl.BlockSpec(memory_space=pl.ANY)
    vmem = pl.BlockSpec(memory_space=pltpu.VMEM)
    dma = pltpu.SemaphoreType.DMA
    bf16, f32 = jnp.bfloat16, jnp.float32
    width = HEADS * DIM
    moved = (GROUP, 2, DIM, DIM)
    in_hbm = [
        pltpu.with_memory_space_constraint(a, pltpu.HBM)
        for a in (queries, key_rows, value_rows, slopes, parents, lengths, parent_states)
    ]
    att, child = pl.pallas_call(
        exchange,
        out_shape=(
            jax.ShapeDtypeStruct((SEG, width), bf16),
            jax.ShapeDtypeStruct(moved, f32),
        ),
        in_specs=[anywhere] * 7,
        out_specs=(vmem,) * 2,
        scratch_shapes=[
            pltpu.VMEM((SEG, width), bf16),
            pltpu.VMEM((SEG, width), bf16),
            pltpu.VMEM((SEG, width), bf16),
            pltpu.SMEM((HEADS,), f32),
            pltpu.SMEM((GROUP,), jnp.int32),
            pltpu.SMEM((GROUP,), jnp.int32),
            pltpu.VMEM((2, 2, DIM, DIM), f32),
            pltpu.VMEM((SEG, width), f32),
            pltpu.VMEM((SEG, SEG), f32),
            pltpu.VMEM(moved, bf16),
            pltpu.VMEM(moved, bf16),
            pltpu.VMEM((2, 2 * SIDE * SIDE, DIM, DIM), bf16),
            pltpu.VMEM((2, 2 * SIDE * SIDE, DIM, DIM), bf16),
            pltpu.VMEM(moved, bf16),
            pltpu.VMEM(moved, bf16),
            pltpu.VMEM(moved, bf16),
            dma((3,)),
            dma((4,)),
            dma((2,)),
            dma((1,)),
            dma((4,)),
            dma((2,)),
            dma((2,)),
            dma((2,)),
            dma((2, LAST + 1)),
        ],
        compiler_params=pltpu.CompilerParams(
            collective_id=0, has_side_effects=True, vmem_limit_bytes=40 * 1024 * 1024
        ),
        name="exchange",
    )(*in_hbm)
    mixed, child = pl.pallas_call(
        settle,
        out_shape=(
            jax.ShapeDtypeStruct((SEG, width), bf16),
            jax.ShapeDtypeStruct(moved, f32),
        ),
        in_specs=[vmem] * 3,
        out_specs=(anywhere,) * 2,
        scratch_shapes=[
            pltpu.VMEM((SEG, width), bf16),
            dma((2,)),
        ],
        compiler_params=pltpu.CompilerParams(vmem_limit_bytes=32 * 1024 * 1024),
        name="settle",
    )(att, child, norm_gain.reshape(1, width))
    return mixed, child


def solution(mesh):
    in_specs = (
        P(("dp", "expert"), None),
        P(("dp", "expert"), None),
        P(("dp", "expert"), None),
        P(),
        P(),
        P("dp"),
        P("dp"),
        P("dp", "expert", None, None),
    )
    out_specs = (P(("dp", "expert"), None), P("dp", "expert", None, None))
    return jax.shard_map(body, mesh=mesh, in_specs=in_specs, out_specs=out_specs, check_vma=False)
```

```python
import jax
import jax.numpy as jnp
from jax import lax
from jax.experimental import pallas as pl
from jax.experimental.pallas import tpu as pltpu
from jax.sharding import PartitionSpec as P

EPS = 1e-06
MESH = pl.DeviceIdType.MESH
SIDE = 4
RING = 8
GROUP = 16
HEADS = 32
DIM = 128
SEG = 256
PAIR = 2 * DIM
CUTS = 4
FAR = 1e9
SWAP = 3
LAST = 6
EARLY, MIDDLE = 10, 22


def ring_step(i):
    j = i // 2
    off = RING // 2 + ((j + 1) // 2) * (1 - 2 * (j % 2))
    return off, (i + 1) % 2


def exchange(
    q_hbm, k_hbm, v_hbm, slopes_hbm, parents_hbm, lengths_hbm, states_hbm,
    att, child,
    q, k, v, slopes, parents, lengths, states, total, offsets, sent_u, got_u, bank_own, bank_far, picked, passed, got_s,
    load_sem, small_sem, bank_send, swap_recv, first_recv, second_recv, u_sem, s_send, s_recv,
):
    me_d = lax.axis_index("dp")
    me_e = lax.axis_index("expert")
    y, x = me_d // SIDE, me_d % SIDE
    z, core = me_e // 2, me_e % 2

    arrays = ((k_hbm, k), (v_hbm, v), (q_hbm, q))

    def load(n, cut):
        rows = pl.ds(cut * (SEG // CUTS), SEG // CUTS)
        src, dst = arrays[n]
        return pltpu.make_async_copy(src.at[rows], dst.at[rows], load_sem.at[n])

    def loaded(n):
        pltpu.make_async_copy(*arrays[n], load_sem.at[n]).wait()

    def along(slot, j):
        return y * SIDE + (x + j) % SIDE if slot % 2 == 0 else ((y + j) % SIDE) * SIDE + x

    barrier = pltpu.get_barrier_semaphore()

    def greet(i, _):
        pl.semaphore_signal(
            barrier, inc=1, device_id=(me_d, (me_e + i) % GROUP), device_id_type=MESH
        )
        return 0

    lax.fori_loop(1, GROUP, greet, 0)
    for slot in range(2):
        for j in range(1, SIDE):
            pl.semaphore_signal(
                barrier, inc=1, device_id=(along(slot, j), me_e), device_id_type=MESH
            )

    smalls = [
        pltpu.make_async_copy(src, dst, small_sem.at[n])
        for n, (src, dst) in enumerate(
            ((states_hbm, states), (slopes_hbm, slopes), (lengths_hbm, lengths), (parents_hbm, parents))
        )
    ]
    for small in smalls:
        small.start()
    for n in range(3):
        for cut in range(CUTS):
            load(n, cut).start()

    smalls[0].wait()

    for slot in range(2):
        for parent in range(2):
            bank_own[slot, 2 * me_d + parent] = states[parent, slot].astype(jnp.bfloat16)

    def head_columns(e, head):
        return pl.ds(pl.multiple_of(e * PAIR + head * DIM, DIM), DIM)

    def device(off, flip):
        return 2 * ((z + off) % RING) + (core + flip) % 2

    def partner(i):
        return device(*ring_step(i))

    def source(i):
        off, flip = ring_step(i)
        return device(RING - off, flip)

    def giver(slot, i):
        n = i // 2
        up = 1 + 7 * n - 2 * n * n
        return device(up + slot * (RING - 2 * up), i % 2)

    def taker(slot, i):
        return giver(1 - slot, i)

    def kept_for(e, slot):
        return (e + 2 * SWAP + slot * (GROUP - 4 * SWAP)) % GROUP

    other = device(0, 1)

    pl.semaphore_wait(barrier, GROUP - 1 + 2 * (SIDE - 1))

    def swap(slot):
        return pltpu.make_async_remote_copy(
            src_ref=bank_own.at[slot, pl.ds(2 * me_d, 2)],
            dst_ref=bank_far.at[slot, pl.ds(2 * me_d, 2)],
            send_sem=bank_send.at[0], recv_sem=swap_recv.at[0],
            device_id=(me_d, device(SWAP if slot else RING - SWAP, 0)), device_id_type=MESH,
        )

    def batch(ref, sem):
        return pltpu.make_async_remote_copy(
            src_ref=ref, dst_ref=ref, send_sem=sem, recv_sem=sem,
            device_id=(me_d, other), device_id_type=MESH,
        )

    swap(0).start()
    swap(1).start()

    banks = (bank_own, bank_far)

    def bank_copy(slot, d, to, sem):
        block = banks[slot // 2].at[slot % 2, pl.ds(2 * d, 2)]
        return pltpu.make_async_remote_copy(
            src_ref=block, dst_ref=block, send_sem=bank_send.at[slot // 2],
            recv_sem=sem, device_id=(to, me_e), device_id_type=MESH,
        )

    def first_hop(slot, j):
        return bank_copy(slot, me_d, along(slot, j), first_recv.at[slot])

    def second_hop(slot, b, j):
        return bank_copy(slot, along(slot, b), along(slot + 1, j), second_recv.at[slot // 2])

    def open_gather(slots):
        for slot in slots:
            for j in range(1, SIDE):
                first_hop(slot, j).start()
        for slot in slots:
            for j in range(1, SIDE):
                second_hop(slot, 0, j).start()

    def pass_on(slots):
        for slot in slots:
            blocks = banks[slot // 2].at[slot % 2, pl.ds(0, 2 * (SIDE - 1))]
            batch(blocks, first_recv.at[slot]).wait_recv()
            for b in range(1, SIDE):
                for j in range(1, SIDE):
                    second_hop(slot, b, j).start()

    def close_gather(n):
        blocks = banks[n].at[:, pl.ds(0, 2 * SIDE * (SIDE - 1))]
        batch(blocks, second_recv.at[n]).wait_recv()

    open_gather((0, 1))

    for small in smalls[1:]:
        small.wait()

    length = lengths[me_e]
    place = lax.broadcasted_iota(jnp.int32, (SEG, DIM), 0)
    remain = (length - 1 - place).astype(jnp.float32)
    inside = place < length
    step_of = (place + 1).astype(jnp.float32)

    def update(e):
        for head in range(2):
            cols = head_columns(e, head)
            slope = slopes[2 * e + head]
            fade = jnp.where(remain >= 0.0, jnp.exp(-slope * jnp.maximum(remain, 0.0)), 0.0)
            keys = (k[:, cols].astype(jnp.float32) * fade).astype(jnp.bfloat16)
            sent_u[e, head] = lax.dot_general(
                keys, v[:, cols], (((0,), (0,)), ((), ())), preferred_element_type=jnp.float32
            ).astype(jnp.bfloat16)

    loaded(0)
    loaded(1)
    update(partner(GROUP - 3))

    def send_u(e):
        return pltpu.make_async_remote_copy(
            src_ref=sent_u.at[e], dst_ref=got_u.at[me_e], send_sem=u_sem.at[0],
            recv_sem=u_sem.at[1], device_id=(me_d, e), device_id_type=MESH,
        )

    def send_own(e, slot, i):
        return pltpu.make_async_remote_copy(
            src_ref=picked.at[e, slot], dst_ref=got_s.at[me_e, slot], send_sem=s_send.at[0],
            recv_sem=s_recv.at[0, i], device_id=(me_d, e), device_id_type=MESH,
        )

    def send_far(e, slot, i):
        owner = kept_for(me_e, slot)
        return pltpu.make_async_remote_copy(
            src_ref=passed.at[e, slot], dst_ref=got_s.at[owner, slot], send_sem=s_send.at[1],
            recv_sem=s_recv.at[1, i], device_id=(me_d, e), device_id_type=MESH,
        )

    def update_step(i, _):
        send_u(partner(GROUP - 3 - i)).start()
        update(partner((2 * GROUP - 4 - i) % GROUP))
        return 0

    lax.fori_loop(0, GROUP - 2, update_step, 0)
    update(other)
    send_u(other).start()

    pass_on((0, 1))
    batch(bank_far.at[:, pl.ds(0, 2)], swap_recv.at[0]).wait_recv()
    open_gather((2, 3))

    t_of = lax.broadcasted_iota(jnp.int32, (SEG, SEG), 0)
    s_of = lax.broadcasted_iota(jnp.int32, (SEG, SEG), 1)
    offsets[...] = jnp.where(t_of >= s_of, (t_of - s_of).astype(jnp.float32), FAR)

    loaded(2)

    def within(i, _):
        cols = pl.ds(pl.multiple_of(i * DIM, DIM), DIM)
        decay = jnp.exp(-slopes[i] * offsets[...])
        scores = lax.dot_general(
            q[:, cols], k[:, cols], (((1,), (1,)), ((), ())), preferred_element_type=jnp.float32
        )
        total[:, cols] = jnp.dot(
            (scores * decay).astype(jnp.bfloat16), v[:, cols], preferred_element_type=jnp.float32
        )
        return 0

    lax.fori_loop(0, EARLY, within, 0)
    pass_on((2, 3))
    lax.fori_loop(EARLY, MIDDLE, within, 0)

    def pick(e, _):
        parent = parents[e]
        for slot in range(2):
            picked[e, slot] = bank_own[slot, parent]
        return 0

    def each_other(step):
        def both(i, _):
            for slot in range(2):
                step(slot, i)
            return 0

        lax.fori_loop(0, LAST, both, 0)

    close_gather(0)
    lax.fori_loop(0, GROUP, pick, 0)
    each_other(lambda slot, i: send_own(taker(slot, i), slot, i).start())
    for slot in range(2):
        send_own(other, slot, LAST).start()

    lax.fori_loop(MIDDLE, HEADS, within, 0)

    def grow(e, fresh):
        for head in range(2):
            fade = jnp.exp(
                jnp.full((1, DIM), -slopes[2 * me_e + head] * lengths[e].astype(jnp.float32), jnp.float32)
            )
            child[e, head] = fade * picked[e, head].astype(jnp.float32) + fresh[e, head].astype(
                jnp.float32
            )

    def grow_step(i, _):
        e = source(i)
        grow(e, got_u)
        return 0

    def select(e, slot):
        passed[e, slot] = bank_far[slot, parents[e]]

    def pass_far(slot, i):
        e = giver(slot, i)
        select(e, slot)
        send_far(e, slot, i).start()

    close_gather(1)
    each_other(pass_far)
    for slot in range(2):
        select(other, slot)
        send_far(other, slot, LAST).start()
        select(me_e, slot)

    def finish(owner, slot, src, at):
        cols = head_columns(owner, slot)
        lead = jnp.exp(-slopes[2 * owner + slot] * step_of)
        carried = jnp.dot(q[:, cols], src[at, slot], preferred_element_type=jnp.float32)
        att[:, cols] = jnp.where(inside, total[:, cols] + carried * lead, 0.0).astype(jnp.bfloat16)

    def finish_here(slot, _):
        finish(me_e, slot, picked, me_e)
        finish(kept_for(me_e, slot), slot, passed, me_e)
        return 0

    def arrived(kind, i):
        batch(got_s.at[0], s_recv.at[kind, i]).wait_recv()

    def finish_other(slot, _):
        for owner in (other, kept_for(other, slot)):
            finish(owner, slot, got_s, owner)
        return 0

    def finish_own(i, _):
        arrived(0, i)
        for slot in range(2):
            owner = giver(slot, i)
            finish(owner, slot, got_s, owner)
        return 0

    def finish_far(i, _):
        arrived(1, i)
        for slot in range(2):
            owner = kept_for(taker(slot, i), slot)
            finish(owner, slot, got_s, owner)
        return 0

    lax.fori_loop(0, 2, finish_here, 0)
    batch(bank_own, bank_send.at[0]).wait_send()
    batch(bank_far.at[:, pl.ds(0, 2 * SIDE * SIDE - 2)], bank_send.at[1]).wait_send()
    batch(sent_u.at[pl.ds(0, GROUP - 1)], u_sem.at[0]).wait_send()
    batch(got_u.at[pl.ds(0, GROUP - 1)], u_sem.at[1]).wait_recv()
    grow(me_e, sent_u)
    lax.fori_loop(0, GROUP - 1, grow_step, 0)
    for kind in range(2):
        arrived(kind, LAST)
    lax.fori_loop(0, 2, finish_other, 0)
    lax.fori_loop(0, LAST, finish_own, 0)
    batch(picked.at[pl.ds(0, LAST + 1)], s_send.at[0]).wait_send()
    lax.fori_loop(0, LAST, finish_far, 0)
    batch(passed.at[pl.ds(0, LAST + 1)], s_send.at[1]).wait_send()


STEPS = 4
TOKENS = SEG // STEPS


def settle(att, child, gain, mixed_hbm, child_hbm, mixed, sem):
    kids = GROUP // STEPS

    def child_out(at):
        part = pl.ds(at * kids, kids)
        return pltpu.make_async_copy(child.at[part], child_hbm.at[part], sem.at[0])

    def mixed_out(at):
        part = pl.ds(at * TOKENS, TOKENS)
        return pltpu.make_async_copy(mixed.at[part], mixed_hbm.at[part], sem.at[1])

    def step(at, _):
        here = pl.ds(pl.multiple_of(at * TOKENS, TOKENS), TOKENS)
        rows = att[here, :].astype(jnp.float32)
        mean = jnp.mean(rows * rows, axis=-1, keepdims=True)
        mixed[here, :] = (rows * lax.rsqrt(mean + EPS) * gain[...]).astype(jnp.bfloat16)
        mixed_out(at).start()
        return 0

    for at in range(STEPS):
        child_out(at).start()
    lax.fori_loop(0, STEPS, step, 0)
    pltpu.make_async_copy(child, child_hbm, sem.at[0]).wait()
    pltpu.make_async_copy(mixed, mixed_hbm, sem.at[1]).wait()


def body(queries, key_rows, value_rows, slopes, norm_gain, parents, lengths, parent_states):
    anywhere = pl.BlockSpec(memory_space=pl.ANY)
    vmem = pl.BlockSpec(memory_space=pltpu.VMEM)
    dma = pltpu.SemaphoreType.DMA
    bf16, f32 = jnp.bfloat16, jnp.float32
    width = HEADS * DIM
    moved = (GROUP, 2, DIM, DIM)
    in_hbm = [
        pltpu.with_memory_space_constraint(a, pltpu.HBM)
        for a in (queries, key_rows, value_rows, slopes, parents, lengths, parent_states)
    ]
    att, child = pl.pallas_call(
        exchange,
        out_shape=(
            jax.ShapeDtypeStruct((SEG, width), bf16),
            jax.ShapeDtypeStruct(moved, f32),
        ),
        in_specs=[anywhere] * 7,
        out_specs=(vmem,) * 2,
        scratch_shapes=[
            pltpu.VMEM((SEG, width), bf16),
            pltpu.VMEM((SEG, width), bf16),
            pltpu.VMEM((SEG, width), bf16),
            pltpu.SMEM((HEADS,), f32),
            pltpu.SMEM((GROUP,), jnp.int32),
            pltpu.SMEM((GROUP,), jnp.int32),
            pltpu.VMEM((2, 2, DIM, DIM), f32),
            pltpu.VMEM((SEG, width), f32),
            pltpu.VMEM((SEG, SEG), f32),
            pltpu.VMEM(moved, bf16),
            pltpu.VMEM(moved, bf16),
            pltpu.VMEM((2, 2 * SIDE * SIDE, DIM, DIM), bf16),
            pltpu.VMEM((2, 2 * SIDE * SIDE, DIM, DIM), bf16),
            pltpu.VMEM(moved, bf16),
            pltpu.VMEM(moved, bf16),
            pltpu.VMEM(moved, bf16),
            dma((3,)),
            dma((4,)),
            dma((2,)),
            dma((1,)),
            dma((4,)),
            dma((2,)),
            dma((2,)),
            dma((2,)),
            dma((2, LAST + 1)),
        ],
        compiler_params=pltpu.CompilerParams(
            collective_id=0, has_side_effects=True, vmem_limit_bytes=40 * 1024 * 1024
        ),
        name="exchange",
    )(*in_hbm)
    mixed, child = pl.pallas_call(
        settle,
        out_shape=(
            jax.ShapeDtypeStruct((SEG, width), bf16),
            jax.ShapeDtypeStruct(moved, f32),
        ),
        in_specs=[vmem] * 3,
        out_specs=(anywhere,) * 2,
        scratch_shapes=[
            pltpu.VMEM((SEG, width), bf16),
            dma((2,)),
        ],
        compiler_params=pltpu.CompilerParams(vmem_limit_bytes=32 * 1024 * 1024),
        name="settle",
    )(att, child, norm_gain.reshape(1, width))
    return mixed, child


def solution(mesh):
    in_specs = (
        P(("dp", "expert"), None),
        P(("dp", "expert"), None),
        P(("dp", "expert"), None),
        P(),
        P(),
        P("dp"),
        P("dp"),
        P("dp", "expert", None, None),
    )
    out_specs = (P(("dp", "expert"), None), P("dp", "expert", None, None))
    return jax.shard_map(body, mesh=mesh, in_specs=in_specs, out_specs=out_specs, check_vma=False)
```
